512 devices in a mesh: phase: 16 (over z_lo, core), head: 32 (over x, y, z_hi).
Axes of the slice: x: 4, y: 4, z: 16 (z_hi: 2, z_lo: 8; z = z_hi * 8 + z_lo), core: 2. Of those that a mesh axis runs over, the one named last changes fastest.
Arguments:
- handoff: bfloat16 [16, 256, 8192], P('phase', 'head'), may hold values from -1.5 to 1.5
- segment_ids: int32 [16, 256], P('phase'), may hold values from 0 to 3, never falling along the last dimension, each value on 1 to 128 neighbouring positions
- norm_gain: bfloat16 [16, 8192], P('phase'), may hold values from 0.25 to 1.75
- query_weight: bfloat16 [16, 8192, 4096], P('phase', None, 'head'), may hold values from -1 to 1
- kv_weight: bfloat16 [16, 8192, 1024], P('phase', None, 'head'), may hold values from -1 to 1
- rotation: bfloat16 [16, 32, 128, 128], P('phase', 'head'), may hold values from -2 to 2
- out_weight: bfloat16 [16, 4096, 8192], P('phase', 'head'), may hold values from -0.09375 to 0.09375
- target: bfloat16 [16, 256, 8192], P('phase', 'head'), may hold values from -3 to 3
Outputs:
- passed: bfloat16 [16, 256, 8192], P('phase', 'head')
- rot_grad: float32 [16, 32, 128, 128], P('phase', 'head')
The draws below stay inside these ranges and needn't reach their ends.
Inputs may be any that keep to these rules, and one draw needn't show every extreme that they name: `segment_ids`: segment ids of each micro-batch start at 0 and never fall along the tokens.
All inputs are finite; a program needn't handle non-finite values.
Results may differ from the reference program's by a relative error of at most 0.03.
Values may be sent and summed in bfloat16 or wider, within the bound.
No kernel may reach another device: no remote copies, remote signals or barrier semaphores. Data moves between devices by JAX's collectives and lax.ppermute only.
A program may use at most 64 MiB of HBM per device.

```python
import math
import jax
import jax.numpy as jnp
import numpy as np
from jax import lax

D = 8192
HD = 128
GROUP = 8
TOKENS = 256
QH = 32
KVH = 4
PHASES = 16


def draw_query_weight(key, part):
    key = jax.random.fold_in(key, 11)
    base_key = jax.random.fold_in(key, 0)
    base = jax.random.truncated_normal(base_key, -6.0, 6.0, (PHASES, D, QH * HD), jnp.float32) / math.sqrt(D)
    return base.astype(jnp.bfloat16)


def draw_kv_weight(key, part):
    key = jax.random.fold_in(key, 23)
    base_key = jax.random.fold_in(key, 0)
    base = jax.random.truncated_normal(base_key, -6.0, 6.0, (PHASES, D, 2 * KVH * HD), jnp.float32) / math.sqrt(D)
    return base.astype(jnp.bfloat16)


def draw_rotation(key, part):
    key = jax.random.fold_in(key, 37)
    eye = jnp.eye(HD, dtype=jnp.float32)[None, None, :, :]
    noise = jax.random.truncated_normal(key, -4.0, 4.0, (PHASES, QH, HD, HD), jnp.float32)
    return (eye + noise * (0.5 / math.sqrt(HD))).astype(jnp.bfloat16)


def shard_levels(rng, dims, cuts, least, largest):
    def one(position, blocks):
        draws = jax.random.uniform(jax.random.fold_in(jax.random.fold_in(rng, 6), position), (blocks,), jnp.float32, least / len(cuts), largest / len(cuts))
        return jnp.repeat(jnp.exp(draws), dims[position] // blocks).reshape((-1,) + (1,) * (len(dims) - position - 1))

    factor_of = one(*cuts[0])
    for cut in cuts[1:]:
        factor_of = factor_of * one(*cut)
    return factor_of


def length_profile(number_of, total, reach, skew):
    loads = [(1 << 20) // math.isqrt(grade ** skew) + 1 for grade in range(2, number_of + 1)]
    rest, given = total - reach - (number_of - 1), [1] * (number_of - 1)
    while rest > 0:
        movable = [i for i in range(number_of - 1) if given[i] < reach]
        whole, budget = sum([loads[i] for i in movable]), rest
        for i in movable:
            addition = min(reach - given[i], max(1, budget * loads[i] // whole), rest)
            given[i] = given[i] + addition
            rest = rest - addition
    return np.array([reach] + given)


def uneven(key, count, total, limit, slope):
    if count == 2:
        one = jax.random.randint(key, (), max(1, total - limit), min(limit, total - 1) + 1)
        return jnp.stack([one, total - one])
    tallies = jnp.asarray(length_profile(count, total, limit, slope), jnp.int32)
    pairs = (count - 1) // 2
    source_of, receiver = tallies[1:1 + 2 * pairs:2], tallies[2:2 + 2 * pairs:2]
    margin = jnp.minimum(source_of - 1, limit - receiver)
    shifted = jax.random.randint(jax.random.fold_in(key, 1), (pairs,), 0, 1 << 20) % (margin + 1)
    tallies = tallies.at[1:1 + 2 * pairs:2].set(source_of - shifted).at[2:2 + 2 * pairs:2].set(receiver + shifted)
    return tallies[jax.random.permutation(jax.random.fold_in(key, 2), count)]


def normal_values(own_key, shape, spread, limit, cuts=(), kind=jnp.bfloat16):
    drawn = jax.random.normal(own_key, shape, jnp.float32) * spread
    if len(cuts) > 0:
        drawn = shard_levels(own_key, shape, cuts, -0.22, 0.18) * drawn
    return jnp.clip(drawn, min=-limit, max=limit).astype(kind)


def setup_inputs(seed: int = 0) -> dict:
    splits = jax.random.split(jax.random.key(seed), 9)
    return {
        "handoff": normal_values(splits[0], (PHASES, TOKENS, D), 0.25, 1.5, ((0, 16), (1, 32))),
        "segment_ids": jax.vmap(lambda own: jnp.searchsorted(jnp.cumsum(uneven(own, 4, TOKENS, TOKENS // 2, 1)), jnp.arange(TOKENS), side="right"))(jax.random.split(splits[1], PHASES)).reshape((PHASES, TOKENS)).astype(jnp.int32),
        "norm_gain": jnp.clip(1.0 + 0.15 * jax.random.normal(splits[2], (PHASES, D), jnp.float32), 0.25, 1.75).astype(jnp.bfloat16),
        "query_weight": draw_query_weight(jax.random.fold_in(splits[8], 71), 0),
        "kv_weight": draw_kv_weight(jax.random.fold_in(splits[8], 71), 0),
        "rotation": draw_rotation(jax.random.fold_in(splits[8], 71), 0),
        "out_weight": normal_values(splits[6], (PHASES, QH * HD, D), (QH * HD) ** -0.5, 0.09375, ((0, 16), (1, 32))),
        "target": normal_values(splits[7], (PHASES, TOKENS, D), 0.5, 3.0, ((0, 16), (1, 32))),
    }


rope_base = 500000.0
masked_score = -1e+30

def normalize(block, gain):
    wide = block.astype(jnp.float32)
    scale = lax.rsqrt(lax.optimization_barrier(jnp.mean(wide * wide, axis=-1, keepdims=True)) + 1e-05)
    return (wide * scale * gain.astype(jnp.float32)).astype(jnp.bfloat16)

def rotate_pairs(values, positions, first):
    width = values.shape[1]
    pair = (first + jnp.arange(width, dtype=jnp.int32)) // 2
    freq = jnp.power(rope_base, -(2.0 * pair.astype(jnp.float32)) / HD)
    angle = positions[:, None] * freq[None, :]
    cosine = jnp.cos(angle[:, 0::2])
    sine = jnp.sin(angle[:, 0::2])
    even = values[:, 0::2]
    odd = values[:, 1::2]
    joined = jnp.stack([even * cosine - odd * sine, even * sine + odd * cosine], axis=-1)
    return joined.reshape(values.shape)

def positions_and_mask(segments):
    count = segments.shape[0]
    order = jnp.arange(count, dtype=jnp.int32)
    same = segments[:, None] == segments[None, :]
    earlier = order[None, :] < order[:, None]
    positions = lax.optimization_barrier(jnp.sum((same & earlier).astype(jnp.int32), axis=1)).astype(jnp.float32)
    allowed = same & (order[None, :] <= order[:, None])
    return (positions, allowed)

def attend(query, key_block, value_block, allowed):
    scores = jnp.dot(query, key_block.T, preferred_element_type=jnp.float32) * HD ** (-0.5)
    scores = jnp.where(allowed, scores, masked_score)
    peak = lax.optimization_barrier(jnp.max(scores, axis=1, keepdims=True))
    powers = jnp.where(allowed, jnp.exp(scores - peak), 0.0)
    prob = (powers / lax.optimization_barrier(jnp.sum(powers, axis=1, keepdims=True))).astype(jnp.bfloat16)
    return jnp.dot(prob, value_block, preferred_element_type=jnp.float32).astype(jnp.bfloat16)

def one_phase(inputs):
    rows, segments, gain, w_query, w_pair, rotations, w_out, goal = inputs
    positions, allowed = positions_and_mask(segments)
    normed = normalize(rows, gain)
    query_all = jnp.dot(normed, w_query, preferred_element_type=jnp.float32)
    pair_all = jnp.dot(normed, w_pair, preferred_element_type=jnp.float32).reshape(TOKENS, KVH, 2, HD)
    keys = jax.vmap(lambda block: rotate_pairs(block, positions, 0), in_axes=1, out_axes=1)(pair_all[:, :, 0, :]).astype(jnp.bfloat16)
    values = pair_all[:, :, 1, :].astype(jnp.bfloat16)

    def head_step(total, head):
        query = rotate_pairs(lax.dynamic_slice_in_dim(query_all, head * HD, HD, 1), positions, 0).astype(jnp.bfloat16)
        group = head // GROUP
        key_block = lax.dynamic_index_in_dim(keys, group, 1, keepdims=False)
        value_block = lax.dynamic_index_in_dim(values, group, 1, keepdims=False)
        mixed = attend(query, key_block, value_block, allowed)
        turn = lax.dynamic_index_in_dim(rotations, head, 0, keepdims=False)
        turned = jnp.dot(mixed, turn, preferred_element_type=jnp.float32).astype(jnp.bfloat16)
        out_rows = lax.dynamic_slice_in_dim(w_out, head * HD, HD, 0)
        term = lax.optimization_barrier(jnp.dot(turned, out_rows, preferred_element_type=jnp.float32).astype(jnp.bfloat16))
        return (total + term.astype(jnp.float32), mixed)
    total, mixed_all = lax.scan(head_step, jnp.zeros((TOKENS, D), jnp.float32), jnp.arange(QH, dtype=jnp.int32))
    passed = (rows.astype(jnp.float32) + total).astype(jnp.bfloat16)
    error = (passed.astype(jnp.float32) - goal.astype(jnp.float32)).astype(jnp.bfloat16)
    back = lax.dot_general(error, w_out, (((1,), (1,)), ((), ())), preferred_element_type=jnp.float32).astype(jnp.bfloat16)
    back = back.reshape(TOKENS, QH, HD)
    grad = jnp.einsum('htd,the->hde', mixed_all.astype(jnp.float32), back.astype(jnp.float32))
    return (passed, grad)

def reference(handoff, segment_ids, norm_gain, query_weight, kv_weight, rotation, out_weight, target):
    arriving = jnp.roll(handoff, 1, axis=0)
    passed, rot_grad = lax.map(one_phase, (arriving, segment_ids, norm_gain, query_weight, kv_weight, rotation, out_weight, target))
    return (passed, rot_grad)
```

```python
import jax
import jax.numpy as jnp
from jax import lax
from jax.sharding import Mesh, PartitionSpec as P

HD = 128
NX, NY, NZ = 4, 4, 2
PIECE = 32
bf16 = jnp.bfloat16
f32 = jnp.float32
rope_base = 500000.0
masked_score = -1e30
EVERY = ("phase", "x", "y", "z")


def relay(block, flip):
    phases = lax.axis_size("phase")
    heads = NX * NY * NZ
    pairs = [
        (p * heads + h, (p + 1) % phases * heads + (h ^ flip)) for p in range(phases) for h in range(heads)
    ]
    return lax.ppermute(block, EVERY, pairs)


def z_swap(block):
    return lax.ppermute(block, "z", [(0, 1), (1, 0)])


def exchange(blocks, axes):
    return lax.all_to_all(blocks, axes, 0, 0, tiled=True)


def in_z_order(own, other, place):
    first = jnp.where(place == 0, own, other)
    second = jnp.where(place == 0, other, own)
    return first, second


def normalize(block, gain):
    wide = block.astype(f32)
    scale = lax.rsqrt(jnp.mean(wide * wide, axis=-1, keepdims=True) + 1e-05)
    return (wide * scale * gain.astype(f32)).astype(bf16)


def tables(positions):
    lane = jnp.arange(HD, dtype=jnp.int32)
    pair = lane // 2
    freq = jnp.power(rope_base, -(2.0 * pair.astype(f32)) / HD)
    angle = positions[:, None] * freq[None, :]
    sine = jnp.sin(angle)
    return jnp.cos(angle), jnp.where(lane[None, :] % 2 == 0, -sine, sine)


def rotate(values, cosine, signed_sine):
    lane = jnp.arange(HD, dtype=jnp.int32)[None, :]
    swapped = jnp.where(lane % 2 == 0, jnp.roll(values, -1, axis=1), jnp.roll(values, 1, axis=1))
    return values * cosine + swapped * signed_sine


def positions_and_mask(segments):
    count = segments.shape[0]
    order = jnp.arange(count, dtype=jnp.int32)
    same = segments[:, None] == segments[None, :]
    earlier = order[None, :] < order[:, None]
    positions = jnp.sum((same & earlier).astype(jnp.int32), axis=1).astype(f32)
    allowed = same & (order[None, :] <= order[:, None])
    return (positions, allowed)


def attend(query, key_block, value_block, allowed):
    scores = jnp.dot(query, key_block.T, preferred_element_type=f32) * HD ** (-0.5)
    scores = jnp.where(allowed, scores, masked_score)
    peak = jnp.max(scores, axis=1, keepdims=True)
    powers = jnp.where(allowed, jnp.exp(scores - peak), 0.0)
    prob = (powers / jnp.sum(powers, axis=1, keepdims=True)).astype(bf16)
    return jnp.dot(prob, value_block, preferred_element_type=f32).astype(bf16)


def local(handoff, segment_ids, norm_gain, query_weight, kv_weight, rotation, out_weight, target):
    segments = segment_ids[0]
    gain = norm_gain[0]
    w_query = query_weight[0]
    w_pair = kv_weight[0]
    w_out = out_weight[0]
    width = gain.shape[0]
    part = width // NY
    rows = handoff.shape[1]
    tokens = segments.shape[0]
    place = lax.axis_index("z")

    x_pair = jnp.concatenate(in_z_order(relay(handoff[0], 0), relay(handoff[0], 1), place), axis=0)
    goal_pair = jnp.concatenate(in_z_order(target[0], z_swap(target[0]), place), axis=0)

    wq_ring = exchange(w_query.reshape(NY, part, HD), "y")
    wkv_ring = exchange(w_pair.T.reshape(PIECE, NY, part).transpose(1, 0, 2), "y").reshape(NY * PIECE, part)
    wkv_other = z_swap(wkv_ring)
    wo_ring = exchange(w_out.reshape(HD, NX, part).transpose(1, 0, 2), "x").reshape(NX * HD, part)

    positions, allowed = positions_and_mask(segments)
    cosine, sine = tables(positions)

    xn = normalize(x_pair, gain).reshape(2 * rows, NY, part).transpose(1, 0, 2)
    xn = exchange(jnp.broadcast_to(xn[None], (NX, NY, 2 * rows, part)).reshape(NX * NY, 2 * rows, part), ("x", "y"))
    xn = xn.reshape(tokens, part)
    raw = jnp.stack([x_pair, goal_pair]).reshape(4 * rows, NX, part).transpose(1, 0, 2)
    raw = exchange(raw, "x").reshape(NX, 2, 2 * rows, part)
    x_slice = raw[:, 0].reshape(NX * 2 * rows, part)
    goal_slice = raw[:, 1].reshape(NX * 2 * rows, part)

    q_part = lax.dot_general(xn, wq_ring, (((1,), (1,)), ((), ())), preferred_element_type=f32).astype(bf16)
    kv_own = lax.dot_general(xn, wkv_ring, (((1,), (1,)), ((), ())), preferred_element_type=f32).astype(bf16)
    kv_other = lax.dot_general(xn, wkv_other, (((1,), (1,)), ((), ())), preferred_element_type=f32).astype(bf16)
    even, odd = in_z_order(kv_own, kv_other, place)
    kv_part = jnp.stack([even.reshape(tokens, NY, PIECE), odd.reshape(tokens, NY, PIECE)], axis=2).reshape(tokens, 2 * HD)
    sent = jnp.concatenate(
        [q_part.transpose(1, 0, 2), jnp.broadcast_to(kv_part[None], (NY, tokens, 2 * HD))], axis=2
    )
    summed = jnp.sum(exchange(sent, "y").astype(f32), axis=0)
    query = rotate(summed[:, :HD], cosine, sine).astype(bf16)
    key_block = rotate(summed[:, HD : 2 * HD], cosine, sine).astype(bf16)
    value_block = summed[:, 2 * HD :].astype(bf16)
    mixed = attend(query, key_block, value_block, allowed)
    turned = jnp.dot(mixed, rotation[0, 0], preferred_element_type=f32).astype(bf16)

    both = jnp.concatenate([mixed, turned], axis=1)
    both = both.reshape(NX, NY, 2 * rows, 2 * HD).transpose(1, 0, 2, 3).reshape(tokens, 2 * HD)
    both = exchange(jnp.broadcast_to(both[None], (NX, tokens, 2 * HD)), "x")
    mixed_ring = both[:, :, :HD]
    turned_ring = both[:, :, HD:].transpose(1, 0, 2).reshape(tokens, NX * HD)
    terms = jnp.dot(turned_ring, wo_ring, preferred_element_type=f32).astype(bf16)
    terms = exchange(terms.reshape(NY, tokens // NY, part), "y")
    half = jnp.sum(terms.astype(f32), axis=0).astype(bf16)
    total = half.astype(f32) + z_swap(half).astype(f32)
    passed = (x_slice.astype(f32) + total).astype(bf16)
    error = (passed.astype(f32) - goal_slice.astype(f32)).astype(bf16)
    error_all = exchange(jnp.broadcast_to(error[None], (NY,) + error.shape), "y").reshape(tokens, part)
    back = lax.dot_general(error_all, wo_ring, (((1,), (1,)), ((), ())), preferred_element_type=f32).astype(bf16)
    grads = jnp.stack(
        [
            lax.dot_general(
                mixed_ring[i],
                back[:, i * HD : (i + 1) * HD],
                (((0,), (0,)), ((), ())),
                preferred_element_type=f32,
            )
            for i in range(NX)
        ]
    ).astype(bf16)
    own_rows = lax.dynamic_slice_in_dim(passed.reshape(NX, NZ, rows, part), place, 1, 1)
    own_rows = own_rows.reshape(NX, rows * part // HD, HD)
    last = exchange(jnp.concatenate([grads, own_rows], axis=1), "x")
    rot_grad = jnp.sum(last[:, :HD].astype(f32), axis=0)
    out_rows = last[:, HD:].reshape(NX, rows, part).transpose(1, 0, 2).reshape(rows, width)
    return (out_rows[None], rot_grad[None, None])


def solution(mesh):
    devices = mesh.devices
    grid = Mesh(devices.reshape(devices.shape[0], NX, NY, NZ), EVERY)
    head = ("x", "y", "z")
    in_specs = (
        P("phase", head, None),
        P("phase", None),
        P("phase", None),
        P("phase", None, head),
        P("phase", None, head),
        P("phase", head, None, None),
        P("phase", head, None),
        P("phase", head, None),
    )
    out_specs = (P("phase", head, None), P("phase", head, None, None))
    return jax.shard_map(local, mesh=grid, in_specs=in_specs, out_specs=out_specs, check_vma=False)
```

```python
import jax
import jax.numpy as jnp
from jax import lax
from jax.experimental import pallas as pl
from jax.experimental.pallas import tpu as pltpu
from jax.sharding import Mesh, PartitionSpec as P

HD = 128
NX, NY, NZ = 4, 4, 2
PLANE = NX * NY
PIECE = 32
TOK = 256
ROWS = 8
D = 8192
PART = D // NY
FINE = D // PLANE
TILES = FINE // HD
bf16 = jnp.bfloat16
f32 = jnp.float32
rope_base = 500000.0
masked_score = -1e30
EVERY = ("phase", "x", "y", "z")
VMEM = pl.BlockSpec(memory_space=pltpu.VMEM)
SMEM = pl.BlockSpec(memory_space=pltpu.SMEM)
HELD = pl.BlockSpec(memory_space=pl.ANY)


def on_core(body, out_shape, in_specs, flops, moved, scratch=(), out_specs=VMEM):
    return pl.pallas_call(
        body,
        out_shape=out_shape,
        in_specs=in_specs,
        out_specs=out_specs,
        scratch_shapes=list(scratch),
        compiler_params=pltpu.CompilerParams(vmem_limit_bytes=40 * 2**20),
        cost_estimate=pl.CostEstimate(flops=flops, bytes_accessed=moved, transcendentals=0),
    )


def dot(a, b, dims=((1,), (0,))):
    return lax.dot_general(a, b, (dims, ((), ())), preferred_element_type=f32)


def relay(block, flip):
    phases = lax.axis_size("phase")
    heads = PLANE * NZ
    pairs = [
        (p * heads + h, (p + 1) % phases * heads + (h ^ flip)) for p in range(phases) for h in range(heads)
    ]
    return lax.ppermute(block, EVERY, pairs)


def z_swap(block):
    return lax.ppermute(block, "z", [(0, 1), (1, 0)])


def exchange(blocks, axes):
    return lax.all_to_all(blocks, axes, 0, 0, tiled=True)


def fine_column(place):
    return place % NY * PART + place // NY * FINE


def pack_kv_body(w_ref, out_ref):
    for y in range(NY):
        block = w_ref[:, y * PART : (y + 1) * PART]
        for z in range(NZ):
            out_ref[y * NZ + z] = block


def pack_out_body(w_ref, turn_ref, after_ref, out_ref):
    for place in range(PLANE):
        start = fine_column(place)
        out_ref[place, :, :FINE] = w_ref[:, start : start + FINE]
        out_ref[place, :, FINE:] = turn_ref[...]


def pack_rows_body(z_ref, own_ref, other_ref, out_ref):
    own = own_ref[...].astype(f32)
    other = other_ref[...].astype(f32)
    at_zero = z_ref[0] == 0
    wide = jnp.concatenate([jnp.where(at_zero, own, other), jnp.where(at_zero, other, own)], axis=0)
    scale = lax.rsqrt(jnp.mean(wide * wide, axis=-1, keepdims=True) + 1e-05)
    high = scale.astype(bf16).astype(f32)
    lane = lax.broadcasted_iota(jnp.int32, (2 * ROWS, HD), 1)
    tail = jnp.where(lane < HD // 2, high, scale - high).astype(bf16)
    narrow = wide.astype(bf16)
    for place in range(PLANE):
        y = place % NY
        out_ref[place, :, :PART] = narrow[:, y * PART : (y + 1) * PART]
        out_ref[place, :, PART:] = tail


def project_body(x_ref, gain_ref, wq_ref, wkv_ref, out_ref):
    tail = x_ref[:, PART:].astype(f32)
    scale = tail[:, 0:1] + tail[:, HD // 2 : HD // 2 + 1]
    normed = (x_ref[:, :PART].astype(f32) * scale * gain_ref[...].astype(f32)).astype(bf16)
    pair = dot(normed, wkv_ref[...], ((1,), (1,))).astype(bf16)
    for y in range(NY):
        out_ref[y, :, :HD] = dot(normed, wq_ref[y]).astype(bf16)
        out_ref[y, :, HD:] = pair


def rotate(values, cosine, signed_sine):
    lane = lax.broadcasted_iota(jnp.int32, values.shape, 1)
    swapped = jnp.where(lane % 2 == 0, jnp.roll(values, -1, axis=1), jnp.roll(values, 1, axis=1))
    return values * cosine + swapped * signed_sine


def attend_body(z_ref, got_ref, cosine_ref, sine_ref, down_ref, across_ref, goal_ref, goal_other_ref, out_ref):
    total = got_ref[0].astype(f32)
    for y in range(1, NY):
        total = total + got_ref[y].astype(f32)
    cosine = cosine_ref[...]
    sine = sine_ref[...]
    query = rotate(total[:, :HD], cosine, sine).astype(bf16)
    key_block = rotate(total[:, HD : 2 * HD], cosine, sine).astype(bf16)
    value_block = total[:, 2 * HD :].astype(bf16)
    scores = dot(query, key_block, ((1,), (1,))) * HD ** (-0.5)
    order = lax.broadcasted_iota(jnp.int32, (TOK, TOK), 0)
    against = lax.broadcasted_iota(jnp.int32, (TOK, TOK), 1)
    allowed = (down_ref[...] == across_ref[...]) & (against <= order)
    scores = jnp.where(allowed, scores, masked_score)
    peak = jnp.max(scores, axis=1, keepdims=True)
    powers = jnp.where(allowed, jnp.exp(scores - peak), 0.0)
    prob = (powers / jnp.sum(powers, axis=1, keepdims=True)).astype(bf16)
    mixed = dot(prob, value_block).astype(bf16)
    at_zero = z_ref[0] == 0
    own = goal_ref[...].astype(f32)
    other = goal_other_ref[...].astype(f32)
    goal = jnp.concatenate([jnp.where(at_zero, own, other), jnp.where(at_zero, other, own)], axis=0).astype(bf16)
    for place in range(PLANE):
        out_ref[place, :TOK] = mixed
        start = fine_column(place)
        for k in range(TILES):
            out_ref[place, TOK + 16 * k : TOK + 16 * k + 16] = goal[:, start + k * HD : start + (k + 1) * HD]


def terms_body(got_ref, w_ref, out_ref):
    total = jnp.zeros((TOK, FINE), f32)
    for place in range(PLANE):
        turned = dot(got_ref[place, :TOK], w_ref[place, :, FINE:]).astype(bf16)
        total = total + dot(turned, w_ref[place, :, :FINE])
    out_ref[...] = total.astype(bf16)


def grads_body(spot_ref, own_ref, other_ref, x_ref, got_ref, w_ref, out_ref, wide_ref):
    start = pl.multiple_of(spot_ref[0] * FINE, FINE)
    raw = x_ref[:, pl.ds(start, FINE)].astype(f32)
    passed = (raw + (own_ref[...].astype(f32) + other_ref[...].astype(f32))).astype(bf16)
    wide = passed.astype(f32)
    wide_ref[...] = wide
    goal = jnp.concatenate(
        [
            jnp.concatenate([got_ref[place, TOK + 16 * k : TOK + 16 * k + 16] for k in range(TILES)], axis=1)
            for place in range(PLANE)
        ],
        axis=0,
    )
    error = (wide - goal.astype(f32)).astype(bf16)
    for place in range(PLANE):
        back = dot(error, w_ref[place, :, :FINE], ((1,), (1,))).astype(bf16)
        out_ref[place, :HD] = dot(got_ref[place, :TOK], back, ((0,), (0,))).astype(bf16)
        first = pl.multiple_of(place * 2 * ROWS + spot_ref[1] * ROWS, ROWS)
        mine = wide_ref[pl.ds(first, ROWS), :]
        stacked = jnp.concatenate([mine[:, k * HD : (k + 1) * HD] for k in range(TILES)], axis=0)
        out_ref[place, HD:] = stacked.astype(bf16)


def finish_body(got_ref, rows_ref, grad_ref):
    total = got_ref[0, :HD].astype(f32)
    for place in range(1, PLANE):
        total = total + got_ref[place, :HD].astype(f32)
    grad_ref[...] = total
    for place in range(PLANE):
        start = fine_column(place)
        stacked = got_ref[place, HD:].astype(f32)
        row = jnp.concatenate([stacked[k * ROWS : (k + 1) * ROWS] for k in range(TILES)], axis=1)
        rows_ref[:, start : start + FINE] = row.astype(bf16)


def tables(segments):
    order = jnp.arange(TOK, dtype=jnp.int32)
    same = segments[:, None] == segments[None, :]
    earlier = order[None, :] < order[:, None]
    positions = jnp.sum((same & earlier).astype(jnp.int32), axis=1).astype(f32)
    lane = jnp.arange(HD, dtype=jnp.int32)
    freq = jnp.power(rope_base, -(2.0 * (lane // 2).astype(f32)) / HD)
    angle = positions[:, None] * freq[None, :]
    sine = jnp.sin(angle)
    return jnp.cos(angle), jnp.where(lane[None, :] % 2 == 0, -sine, sine)


def local(handoff, segment_ids, norm_gain, query_weight, kv_weight, rotation, out_weight, target):
    segments = segment_ids[0]
    w_query = query_weight[0]
    w_pair = kv_weight[0].T
    w_out = out_weight[0]
    goal = target[0]
    x_at, y_at, z_at = lax.axis_index("x"), lax.axis_index("y"), lax.axis_index("z")
    z_flag = z_at.astype(jnp.int32).reshape(1)
    spot = jnp.stack([x_at, z_at]).astype(jnp.int32)
    gain = lax.dynamic_slice_in_dim(norm_gain, y_at * PART, PART, 1)
    cosine, sine = tables(segments)

    own, other = relay(handoff[0], 0), relay(handoff[0], 1)
    wq_ring = exchange(w_query.reshape(NY, PART, HD), "y")
    pair_pack = on_core(
        pack_kv_body,
        jax.ShapeDtypeStruct((NY * NZ, PIECE, PART), bf16),
        [VMEM],
        0,
        3 * 2**19,
    )(w_pair)
    wkv_ring = exchange(pair_pack, ("y", "z")).reshape(2 * HD, PART)

    rows = on_core(
        pack_rows_body,
        jax.ShapeDtypeStruct((PLANE, 2 * ROWS, PART + HD), bf16),
        [SMEM, VMEM, VMEM],
        10**6,
        3 * 2**19,
    )(z_flag, own, other)
    features = exchange(rows, ("x", "y")).reshape(TOK, PART + HD)

    wo_pack = on_core(
        pack_out_body,
        jax.ShapeDtypeStruct((PLANE, HD, FINE + HD), bf16),
        [VMEM, VMEM, HELD],
        0,
        9 * 2**19,
    )(w_out, rotation[0, 0], rows)
    wo_ring = exchange(wo_pack, ("x", "y"))
    goal_other = z_swap(goal)

    sent = on_core(
        project_body,
        jax.ShapeDtypeStruct((NY, TOK, 3 * HD), bf16),
        [VMEM] * 4,
        2 * TOK * PART * 6 * HD,
        5 * 2**20,
    )(features, gain, wq_ring, wkv_ring)
    got = exchange(sent, "y")

    mixed = on_core(
        attend_body,
        jax.ShapeDtypeStruct((PLANE, TOK + 16 * TILES, HD), bf16),
        [SMEM] + [VMEM] * 7,
        10**8,
        3 * 2**20,
    )(z_flag, got, cosine, sine, segments[:, None], segments[None, :], goal, goal_other)
    mixed = exchange(mixed, ("x", "y"))

    terms = on_core(
        terms_body,
        jax.ShapeDtypeStruct((TOK, FINE), bf16),
        [VMEM] * 2,
        2 * TOK * PLANE * HD * (FINE + HD),
        4 * 2**20,
    )(mixed, wo_ring)
    terms_other = z_swap(terms)

    parts = on_core(
        grads_body,
        jax.ShapeDtypeStruct((PLANE, HD + ROWS * TILES, HD), bf16),
        [SMEM] + [VMEM] * 5,
        2 * TOK * PLANE * HD * (FINE + HD),
        6 * 2**20,
        [pltpu.VMEM((TOK, FINE), f32)],
    )(spot, terms, terms_other, features, mixed, wo_ring)
    parts = exchange(parts, ("x", "y"))

    out_rows, rot_grad = on_core(
        finish_body,
        (jax.ShapeDtypeStruct((ROWS, D), bf16), jax.ShapeDtypeStruct((HD, HD), f32)),
        [VMEM],
        10**6,
        2**20,
        out_specs=(VMEM, VMEM),
    )(parts)
    return (out_rows[None], rot_grad[None, None])


def solution(mesh):
    devices = mesh.devices
    grid = Mesh(devices.reshape(devices.shape[0], NX, NY, NZ), EVERY)
    head = ("x", "y", "z")
    in_specs = (
        P("phase", head, None),
        P("phase", None),
        P("phase", None),
        P("phase", None, head),
        P("phase", None, head),
        P("phase", head, None, None),
        P("phase", head, None),
        P("phase", head, None),
    )
    out_specs = (P("phase", head, None), P("phase", head, None, None))
    return jax.shard_map(local, mesh=grid, in_specs=in_specs, out_specs=out_specs, check_vma=False)
```

```python
import jax
import jax.numpy as jnp
from jax import lax
from jax.experimental import pallas as pl
from jax.experimental.pallas import tpu as pltpu
from jax.sharding import Mesh, PartitionSpec as P

HD = 128
NX, NY, NZ = 4, 4, 2
PLANE = NX * NY
PIECE = 32
TOK = 256
ROWS = 8
D = 8192
PART = D // NY
FINE = D // PLANE
TILES = FINE // HD
bf16 = jnp.bfloat16
f32 = jnp.float32
rope_base = 500000.0
masked_score = -1e30
EVERY = ("phase", "x", "y", "z")
VMEM = pl.BlockSpec(memory_space=pltpu.VMEM)
SMEM = pl.BlockSpec(memory_space=pltpu.SMEM)
HELD = pl.BlockSpec(memory_space=pl.ANY)


def on_core(body, out_shape, in_specs, flops, moved, scratch=(), out_specs=VMEM, grid=()):
    return pl.pallas_call(
        body,
        out_shape=out_shape,
        in_specs=in_specs,
        out_specs=out_specs,
        scratch_shapes=list(scratch),
        grid=grid,
        compiler_params=pltpu.CompilerParams(vmem_limit_bytes=40 * 2**20),
        cost_estimate=pl.CostEstimate(flops=flops, bytes_accessed=moved, transcendentals=0),
    )


def dot(a, b, dims=((1,), (0,))):
    return lax.dot_general(a, b, (dims, ((), ())), preferred_element_type=f32)


def relay(block, flip):
    phases = lax.axis_size("phase")
    heads = PLANE * NZ
    pairs = [
        (p * heads + h, (p + 1) % phases * heads + (h ^ flip)) for p in range(phases) for h in range(heads)
    ]
    return lax.ppermute(block, EVERY, pairs)


def z_swap(block):
    return lax.ppermute(block, "z", [(0, 1), (1, 0)])


def y_shift(block, by):
    return lax.ppermute(block, "y", [(y, (y + by) % NY) for y in range(NY)])


def exchange(blocks, axes):
    return lax.all_to_all(blocks, axes, 0, 0, tiled=True)


def fine_column(place):
    return place % NY * PART + place // NY * FINE


def fold(rows):
    return jnp.concatenate([rows[:, k * HD : (k + 1) * HD] for k in range(TILES)], axis=0)


def unfold(rows):
    return jnp.concatenate([rows[k * ROWS : (k + 1) * ROWS] for k in range(TILES)], axis=1)


def pack_in_body(spot_ref, wq_ref, wkv_ref, *out_refs):
    for d in range(NY):
        start = pl.multiple_of((spot_ref[1] + d) % NY * PART, PART)
        out_refs[d][:PART] = wq_ref[pl.ds(start, PART), :]
        for k in range(PART // HD):
            out_refs[d][PART + k * PIECE : PART + (k + 1) * PIECE] = wkv_ref[:, pl.ds(start + k * HD, HD)]


def pack_out_body(w_ref, turn_ref, out_ref):
    for place in range(PLANE):
        start = fine_column(place)
        out_ref[place, :, :FINE] = w_ref[:, start : start + FINE]
        out_ref[place, :, FINE:] = turn_ref[...]


def pack_rows_body(spot_ref, own_ref, other_ref, *refs):
    pieces, (out_ref, pieces_ref) = refs[:NY], refs[-2:]
    for d in range(NY):
        pieces_ref[d] = pieces[d][...]
    own = own_ref[...].astype(f32)
    other = other_ref[...].astype(f32)
    at_zero = spot_ref[2] == 0
    wide = jnp.concatenate([jnp.where(at_zero, own, other), jnp.where(at_zero, other, own)], axis=0)
    scale = lax.rsqrt(jnp.mean(wide * wide, axis=-1, keepdims=True) + 1e-05)
    high = scale.astype(bf16).astype(f32)
    lane = lax.broadcasted_iota(jnp.int32, (2 * ROWS, HD), 1)
    tail = jnp.where(lane < HD // 2, high, scale - high).astype(bf16)
    narrow = wide.astype(bf16)
    for place in range(PLANE):
        y = place % NY
        out_ref[place, :, :PART] = narrow[:, y * PART : (y + 1) * PART]
        out_ref[place, :, PART:] = tail


def project_body(spot_ref, x_ref, gain_ref, w0_ref, w1_ref, w2_ref, w3_ref, across_ref, out_ref, raw_ref, pair_ref):
    rings = (w0_ref, w1_ref, w2_ref, w3_ref)
    raw_ref[...] = x_ref[:, pl.ds(pl.multiple_of(spot_ref[0] * FINE, FINE), FINE)]
    tail = x_ref[:, PART:].astype(f32)
    scale = tail[:, 0:1] + tail[:, HD // 2 : HD // 2 + 1]
    normed = (x_ref[:, :PART].astype(f32) * scale * gain_ref[...].astype(f32)).astype(bf16)
    for d in range(NY):
        base = (spot_ref[1] + NY - d) % NY * (NZ * PIECE)
        own = pl.multiple_of(base + spot_ref[2] * PIECE, PIECE)
        other = pl.multiple_of(base + (1 - spot_ref[2]) * PIECE, PIECE)
        for k in range(PART // HD):
            cut = slice(k * HD, (k + 1) * HD)
            pair_ref[pl.ds(own, PIECE), cut] = rings[d][PART + k * PIECE : PART + (k + 1) * PIECE]
            pair_ref[pl.ds(other, PIECE), cut] = across_ref[d, k * PIECE : (k + 1) * PIECE]
    pair = dot(normed, pair_ref[...], ((1,), (1,))).astype(bf16)
    for d in range(NY):
        y = (spot_ref[1] + NY - d) % NY
        out_ref[y, :, :HD] = dot(normed, rings[d][:PART]).astype(bf16)
        out_ref[y, :, HD:] = pair


def rotate(values, cosine, signed_sine):
    lane = lax.broadcasted_iota(jnp.int32, values.shape, 1)
    swapped = jnp.where(lane % 2 == 0, jnp.roll(values, -1, axis=1), jnp.roll(values, 1, axis=1))
    return values * cosine + swapped * signed_sine


def attend_body(got_ref, cosine_ref, sine_ref, down_ref, across_ref, goal_ref, out_ref):
    total = got_ref[0].astype(f32)
    for y in range(1, NY):
        total = total + got_ref[y].astype(f32)
    cosine = cosine_ref[...]
    sine = sine_ref[...]
    query = rotate(total[:, :HD], cosine, sine).astype(bf16)
    key_block = rotate(total[:, HD : 2 * HD], cosine, sine).astype(bf16)
    value_block = total[:, 2 * HD :].astype(bf16)
    scores = dot(query, key_block, ((1,), (1,))) * HD ** (-0.5)
    order = lax.broadcasted_iota(jnp.int32, (TOK, TOK), 0)
    against = lax.broadcasted_iota(jnp.int32, (TOK, TOK), 1)
    allowed = (down_ref[...] == across_ref[...]) & (against <= order)
    scores = jnp.where(allowed, scores, masked_score)
    peak = jnp.max(scores, axis=1, keepdims=True)
    powers = jnp.where(allowed, jnp.exp(scores - peak), 0.0)
    prob = (powers / jnp.sum(powers, axis=1, keepdims=True)).astype(bf16)
    mixed = dot(prob, value_block).astype(bf16)
    goal = goal_ref[...].astype(f32)
    for place in range(PLANE):
        start = fine_column(place)
        out_ref[place, :TOK] = mixed
        out_ref[place, TOK:] = fold(goal[:, start : start + FINE]).astype(bf16)


def terms_body(spot_ref, got_ref, w_ref, out_ref, sent_ref, goal_ref):
    goal_ref[...] = jnp.zeros((TOK, FINE), f32)
    total = jnp.zeros((TOK, FINE), f32)
    for place in range(PLANE):
        first = pl.multiple_of(place * 2 * ROWS + spot_ref[2] * ROWS, ROWS)
        goal_ref[pl.ds(first, ROWS), :] = unfold(got_ref[place, TOK:].astype(f32))
        turned = dot(got_ref[place, :TOK], w_ref[place, :, FINE:]).astype(bf16)
        total = total + dot(turned, w_ref[place, :, :FINE])
    out_ref[...] = total
    sent_ref[...] = (total - goal_ref[...]).astype(bf16)


def grads_body(spot_ref, own_ref, other_ref, x_ref, goal_ref, got_ref, w_ref, out_ref, wide_ref):
    passed = x_ref[...].astype(f32) + (own_ref[...] + other_ref[...].astype(f32))
    wide = passed.astype(bf16).astype(f32)
    wide_ref[...] = wide
    error = (wide - goal_ref[...]).astype(bf16)
    for place in range(PLANE):
        back = dot(error, w_ref[place, :, :FINE], ((1,), (1,))).astype(bf16)
        out_ref[place, :HD] = dot(got_ref[place, :TOK], back, ((0,), (0,))).astype(bf16)
        first = pl.multiple_of(place * 2 * ROWS + spot_ref[2] * ROWS, ROWS)
        out_ref[place, HD:] = fold(wide_ref[pl.ds(first, ROWS), :]).astype(bf16)


def finish_body(got_ref, rows_ref, grad_ref):
    total = got_ref[0, :HD].astype(f32)
    for place in range(1, PLANE):
        total = total + got_ref[place, :HD].astype(f32)
    grad_ref[...] = total
    for place in range(PLANE):
        start = fine_column(place)
        rows_ref[:, start : start + FINE] = unfold(got_ref[place, HD:].astype(f32)).astype(bf16)


def tables(segments):
    order = jnp.arange(TOK, dtype=jnp.int32)
    same = segments[:, None] == segments[None, :]
    earlier = order[None, :] < order[:, None]
    positions = jnp.sum((same & earlier).astype(jnp.int32), axis=1).astype(f32)
    lane = jnp.arange(HD, dtype=jnp.int32)
    freq = jnp.power(rope_base, -(2.0 * (lane // 2).astype(f32)) / HD)
    angle = positions[:, None] * freq[None, :]
    sine = jnp.sin(angle)
    return jnp.cos(angle), jnp.where(lane[None, :] % 2 == 0, -sine, sine)


def local(handoff, segment_ids, norm_gain, query_weight, kv_weight, rotation, out_weight, target):
    segments = segment_ids[0]
    w_query = query_weight[0]
    w_pair = kv_weight[0].T
    w_out = out_weight[0]
    goal = target[0]
    x_at, y_at, z_at = lax.axis_index("x"), lax.axis_index("y"), lax.axis_index("z")
    spot = jnp.stack([x_at, y_at, z_at]).astype(jnp.int32)
    gain = lax.dynamic_slice_in_dim(norm_gain, y_at * PART, PART, 1)
    cosine, sine = tables(segments)

    own, other = relay(handoff[0], 0), relay(handoff[0], 1)
    depth = PART + PART * PIECE // HD
    rings = on_core(
        pack_in_body,
        (jax.ShapeDtypeStruct((depth, HD), bf16),) * NY,
        [SMEM, VMEM, VMEM],
        0,
        5 * 2**20,
        out_specs=(VMEM,) * NY,
    )(spot, w_query, w_pair)
    rings = [rings[0]] + [y_shift(rings[d], d) for d in range(1, NY)]
    wo_pack = on_core(
        pack_out_body,
        jax.ShapeDtypeStruct((PLANE, HD, FINE + HD), bf16),
        [VMEM, VMEM],
        0,
        9 * 2**19,
    )(w_out, rotation[0, 0])
    wo_ring = exchange(wo_pack, ("x", "y"))

    pieces = pl.BlockSpec((depth - PART, HD), lambda i: (PART // (depth - PART), 0))
    rows, pair_own = on_core(
        pack_rows_body,
        (
            jax.ShapeDtypeStruct((PLANE, 2 * ROWS, PART + HD), bf16),
            jax.ShapeDtypeStruct((NY, depth - PART, HD), bf16),
        ),
        [SMEM, VMEM, VMEM] + [pieces] * NY + [HELD],
        10**6,
        3 * 2**20,
        out_specs=(VMEM, VMEM),
        grid=(1,),
    )(spot, own, other, *rings, wo_ring)
    features = exchange(rows, ("x", "y")).reshape(TOK, PART + HD)
    pair_other = z_swap(pair_own)

    sent, raw = on_core(
        project_body,
        (jax.ShapeDtypeStruct((NY, TOK, 3 * HD), bf16), jax.ShapeDtypeStruct((TOK, FINE), bf16)),
        [SMEM] + [VMEM] * 7,
        2 * TOK * PART * 6 * HD,
        5 * 2**20,
        [pltpu.VMEM((2 * HD, PART), bf16)],
        out_specs=(VMEM, VMEM),
    )(spot, features, gain, *rings, pair_other)
    got = exchange(sent, "y")

    mixed = on_core(
        attend_body,
        jax.ShapeDtypeStruct((PLANE, TOK + ROWS * TILES, HD), bf16),
        [VMEM] * 6,
        10**8,
        3 * 2**20,
    )(got, cosine, sine, segments[:, None], segments[None, :], goal)
    mixed = exchange(mixed, ("x", "y"))

    wide_slice = jax.ShapeDtypeStruct((TOK, FINE), f32)
    terms, terms_sent, goal_slice = on_core(
        terms_body,
        (wide_slice, jax.ShapeDtypeStruct((TOK, FINE), bf16), wide_slice),
        [SMEM, VMEM, VMEM],
        2 * TOK * PLANE * HD * (FINE + HD),
        4 * 2**20,
        out_specs=(VMEM,) * 3,
    )(spot, mixed, wo_ring)
    terms_other = z_swap(terms_sent)

    parts = on_core(
        grads_body,
        jax.ShapeDtypeStruct((PLANE, HD + ROWS * TILES, HD), bf16),
        [SMEM] + [VMEM] * 6,
        2 * TOK * PLANE * HD * (FINE + HD),
        6 * 2**20,
        [pltpu.VMEM((TOK, FINE), f32)],
    )(spot, terms, terms_other, raw, goal_slice, mixed, wo_ring)
    parts = exchange(parts, ("x", "y"))

    out_rows, rot_grad = on_core(
        finish_body,
        (jax.ShapeDtypeStruct((ROWS, D), bf16), jax.ShapeDtypeStruct((HD, HD), f32)),
        [VMEM],
        10**6,
        2**20,
        out_specs=(VMEM, VMEM),
    )(parts)
    return (out_rows[None], rot_grad[None, None])


def solution(mesh):
    devices = mesh.devices
    grid = Mesh(devices.reshape(devices.shape[0], NX, NY, NZ), EVERY)
    head = ("x", "y", "z")
    in_specs = (
        P("phase", head, None),
        P("phase", None),
        P("phase", None),
        P("phase", None, head),
        P("phase", None, head),
        P("phase", head, None, None),
        P("phase", head, None),
        P("phase", head, None),
    )
    out_specs = (P("phase", head, None), P("phase", head, None, None))
    return jax.shard_map(local, mesh=grid, in_specs=in_specs, out_specs=out_specs, check_vma=False)
```

```python
import jax
import jax.numpy as jnp
from jax import lax
from jax.experimental import pallas as pl
from jax.experimental.pallas import tpu as pltpu
from jax.sharding import Mesh, PartitionSpec as P

HD = 128
NX, NY, NZ = 4, 4, 2
PLANE = NX * NY
PIECE = 32
TOK = 256
ROWS = 8
D = 8192
PART = D // NY
FINE = D // PLANE
TILES = FINE // HD
bf16 = jnp.bfloat16
f32 = jnp.float32
rope_base = 500000.0
masked_score = -1e30
EVERY = ("phase", "x", "y", "z")
VMEM = pl.BlockSpec(memory_space=pltpu.VMEM)
SMEM = pl.BlockSpec(memory_space=pltpu.SMEM)
HELD = pl.BlockSpec(memory_space=pl.ANY)


def on_core(body, out_shape, in_specs, flops, moved, scratch=(), out_specs=VMEM):
    return pl.pallas_call(
        body,
        out_shape=out_shape,
        in_specs=in_specs,
        out_specs=out_specs,
        scratch_shapes=list(scratch),
        compiler_params=pltpu.CompilerParams(vmem_limit_bytes=40 * 2**20),
        cost_estimate=pl.CostEstimate(flops=flops, bytes_accessed=moved, transcendentals=0),
    )


def dot(a, b, dims=((1,), (0,))):
    return lax.dot_general(a, b, (dims, ((), ())), preferred_element_type=f32)


def relay(block, flip):
    phases = lax.axis_size("phase")
    heads = PLANE * NZ
    pairs = [
        (p * heads + h, (p + 1) % phases * heads + (h ^ flip)) for p in range(phases) for h in range(heads)
    ]
    return lax.ppermute(block, EVERY, pairs)


def z_swap(block):
    return lax.ppermute(block, "z", [(0, 1), (1, 0)])


def exchange(blocks, axes):
    return lax.all_to_all(blocks, axes, 0, 0, tiled=True)


def fine_column(place):
    return place % NY * PART + place // NY * FINE


def fold(rows):
    return jnp.concatenate([rows[:, k * HD : (k + 1) * HD] for k in range(TILES)], axis=0)


def unfold(rows):
    return jnp.concatenate([rows[k * ROWS : (k + 1) * ROWS] for k in range(TILES)], axis=1)


def pack_in_body(wq_ref, wkv_ref, out_ref):
    for y in range(NY):
        start = y * PART
        out_ref[y, :PART] = wq_ref[start : start + PART]
        for k in range(PART // HD):
            first = PART + k * PIECE
            out_ref[y, first : first + PIECE] = wkv_ref[:, start + k * HD : start + (k + 1) * HD]


def pack_out_body(got_ref, w_ref, turn_ref, pair_ref, out_ref):
    total = got_ref[0, :, HD:].astype(f32)
    for y in range(1, NY):
        total = total + got_ref[y, :, HD:].astype(f32)
    pair_ref[...] = total.astype(bf16)
    for place in range(PLANE):
        start = fine_column(place)
        out_ref[place, :, :FINE] = w_ref[:, start : start + FINE]
        out_ref[place, :, FINE:] = turn_ref[...]


def pack_rows_body(spot_ref, own_ref, other_ref, *refs):
    out_ref = refs[-1]
    own = own_ref[...].astype(f32)
    other = other_ref[...].astype(f32)
    at_zero = spot_ref[2] == 0
    wide = jnp.concatenate([jnp.where(at_zero, own, other), jnp.where(at_zero, other, own)], axis=0)
    scale = lax.rsqrt(jnp.mean(wide * wide, axis=-1, keepdims=True) + 1e-05)
    high = scale.astype(bf16).astype(f32)
    lane = lax.broadcasted_iota(jnp.int32, (2 * ROWS, HD), 1)
    tail = jnp.where(lane < HD // 2, high, scale - high).astype(bf16)
    narrow = wide.astype(bf16)
    for place in range(PLANE):
        y = place % NY
        out_ref[place, :, :PART] = narrow[:, y * PART : (y + 1) * PART]
        out_ref[place, :, PART:] = tail


def project_body(spot_ref, x_ref, gain_ref, ring_ref, out_ref, raw_ref, pair_ref):
    raw_ref[...] = x_ref[:, pl.ds(pl.multiple_of(spot_ref[0] * FINE, FINE), FINE)]
    tail = x_ref[:, PART:].astype(f32)
    scale = tail[:, 0:1] + tail[:, HD // 2 : HD // 2 + 1]
    normed = (x_ref[:, :PART].astype(f32) * scale * gain_ref[...].astype(f32)).astype(bf16)
    for y in range(NY):
        for k in range(PART // HD):
            first = PART + k * PIECE
            pair_ref[y * PIECE : (y + 1) * PIECE, k * HD : (k + 1) * HD] = ring_ref[y, first : first + PIECE]
    pair = dot(normed, pair_ref[...], ((1,), (1,))).astype(bf16)
    for y in range(NY):
        out_ref[y, :, :HD] = dot(normed, ring_ref[y, :PART]).astype(bf16)
        out_ref[y, :, HD:] = pair


def rotate(values, cosine, signed_sine):
    lane = lax.broadcasted_iota(jnp.int32, values.shape, 1)
    swapped = jnp.where(lane % 2 == 0, jnp.roll(values, -1, axis=1), jnp.roll(values, 1, axis=1))
    return values * cosine + swapped * signed_sine


def attend_body(spot_ref, got_ref, own_ref, other_ref, cosine_ref, sine_ref, down_ref, across_ref, goal_ref, held_ref, out_ref):
    total = got_ref[0].astype(f32)
    for y in range(1, NY):
        total = total + got_ref[y].astype(f32)
    own = own_ref[...].astype(f32)
    other = other_ref[...].astype(f32)
    at_zero = spot_ref[2] == 0
    even = jnp.where(at_zero, own, other)
    odd = jnp.where(at_zero, other, own)
    quarter = lax.broadcasted_iota(jnp.int32, (TOK, HD), 1) // PIECE

    def weave(a, b, c, d):
        return jnp.where(quarter == 0, a, jnp.where(quarter == 1, b, jnp.where(quarter == 2, c, d)))

    def turn(values, by):
        return jnp.roll(values, by * PIECE, axis=1)

    keys = weave(even, turn(odd, 1), turn(even, 1), turn(odd, 2))
    value_block = weave(turn(even, 2), turn(odd, 3), turn(even, 3), odd).astype(bf16)
    cosine = cosine_ref[...]
    sine = sine_ref[...]
    query = rotate(total, cosine, sine).astype(bf16)
    key_block = rotate(keys, cosine, sine).astype(bf16)
    scores = dot(query, key_block, ((1,), (1,))) * HD ** (-0.5)
    order = lax.broadcasted_iota(jnp.int32, (TOK, TOK), 0)
    against = lax.broadcasted_iota(jnp.int32, (TOK, TOK), 1)
    allowed = (down_ref[...] == across_ref[...]) & (against <= order)
    scores = jnp.where(allowed, scores, masked_score)
    peak = jnp.max(scores, axis=1, keepdims=True)
    powers = jnp.where(allowed, jnp.exp(scores - peak), 0.0)
    prob = (powers / jnp.sum(powers, axis=1, keepdims=True)).astype(bf16)
    mixed = dot(prob, value_block).astype(bf16)
    goal = goal_ref[...].astype(f32)
    for place in range(PLANE):
        start = fine_column(place)
        out_ref[place, :TOK] = mixed
        out_ref[place, TOK:] = fold(goal[:, start : start + FINE]).astype(bf16)


def terms_body(spot_ref, got_ref, w_ref, out_ref, sent_ref, goal_ref):
    goal_ref[...] = jnp.zeros((TOK, FINE), f32)
    total = jnp.zeros((TOK, FINE), f32)
    for place in range(PLANE):
        first = pl.multiple_of(place * 2 * ROWS + spot_ref[2] * ROWS, ROWS)
        goal_ref[pl.ds(first, ROWS), :] = unfold(got_ref[place, TOK:].astype(f32))
    for place in range(0, PLANE, 2):
        pair = (place, place + 1)
        turned = [dot(got_ref[h, :TOK], w_ref[h, :, FINE:]).astype(bf16) for h in pair]
        weights = jnp.concatenate([w_ref[h, :, :FINE] for h in pair], axis=0)
        total = total + dot(jnp.concatenate(turned, axis=1), weights)
    out_ref[...] = total
    sent_ref[...] = (total - goal_ref[...]).astype(bf16)


def grads_body(spot_ref, own_ref, other_ref, x_ref, goal_ref, got_ref, w_ref, out_ref, wide_ref):
    passed = x_ref[...].astype(f32) + (own_ref[...] + other_ref[...].astype(f32))
    wide = passed.astype(bf16).astype(f32)
    wide_ref[...] = wide
    error = (wide - goal_ref[...]).astype(bf16)
    for place in range(0, PLANE, 2):
        pair = (place, place + 1)
        weights = jnp.concatenate([w_ref[h, :, :FINE] for h in pair], axis=0)
        back = dot(error, weights, ((1,), (1,))).astype(bf16)
        for i, h in enumerate(pair):
            part = dot(got_ref[h, :TOK], back[:, i * HD : (i + 1) * HD], ((0,), (0,)))
            out_ref[h, :HD] = part.astype(bf16)
    for place in range(PLANE):
        first = pl.multiple_of(place * 2 * ROWS + spot_ref[2] * ROWS, ROWS)
        out_ref[place, HD:] = fold(wide_ref[pl.ds(first, ROWS), :]).astype(bf16)


def finish_body(got_ref, rows_ref, grad_ref):
    total = got_ref[0, :HD].astype(f32)
    for place in range(1, PLANE):
        total = total + got_ref[place, :HD].astype(f32)
    grad_ref[...] = total
    for place in range(PLANE):
        start = fine_column(place)
        rows_ref[:, start : start + FINE] = unfold(got_ref[place, HD:].astype(f32)).astype(bf16)


def tables(segments):
    order = jnp.arange(TOK, dtype=jnp.int32)
    same = segments[:, None] == segments[None, :]
    earlier = order[None, :] < order[:, None]
    positions = jnp.sum((same & earlier).astype(jnp.int32), axis=1).astype(f32)
    lane = jnp.arange(HD, dtype=jnp.int32)
    freq = jnp.power(rope_base, -(2.0 * (lane // 2).astype(f32)) / HD)
    angle = positions[:, None] * freq[None, :]
    sine = jnp.sin(angle)
    return jnp.cos(angle), jnp.where(lane[None, :] % 2 == 0, -sine, sine)


def local(handoff, segment_ids, norm_gain, query_weight, kv_weight, rotation, out_weight, target):
    segments = segment_ids[0]
    w_query = query_weight[0]
    w_pair = kv_weight[0].T
    w_out = out_weight[0]
    goal = target[0]
    x_at, y_at, z_at = lax.axis_index("x"), lax.axis_index("y"), lax.axis_index("z")
    spot = jnp.stack([x_at, y_at, z_at]).astype(jnp.int32)
    gain = lax.dynamic_slice_in_dim(norm_gain, y_at * PART, PART, 1)
    cosine, sine = tables(segments)

    down, across = segments[:, None], segments[None, :]

    own, other = relay(handoff[0], 0), relay(handoff[0], 1)
    depth = PART + PART * PIECE // HD
    rings = on_core(
        pack_in_body,
        jax.ShapeDtypeStruct((NY, depth, HD), bf16),
        [VMEM, VMEM],
        0,
        5 * 2**20,
    )(w_query, w_pair)
    rings = exchange(rings, "y")

    rows = on_core(
        pack_rows_body,
        jax.ShapeDtypeStruct((PLANE, 2 * ROWS, PART + HD), bf16),
        [SMEM, VMEM, VMEM] + [HELD] * 4,
        10**6,
        3 * 2**20,
    )(spot, own, other, rings, cosine, sine, down)
    features = exchange(rows, ("x", "y")).reshape(TOK, PART + HD)

    sent, raw = on_core(
        project_body,
        (jax.ShapeDtypeStruct((NY, TOK, 2 * HD), bf16), jax.ShapeDtypeStruct((TOK, FINE), bf16)),
        [SMEM] + [VMEM] * 3,
        2 * TOK * PART * 5 * HD,
        5 * 2**20,
        [pltpu.VMEM((HD, PART), bf16)],
        out_specs=(VMEM, VMEM),
    )(spot, features, gain, rings)
    got = exchange(sent, "y")

    pair_own, wo_pack = on_core(
        pack_out_body,
        (jax.ShapeDtypeStruct((TOK, HD), bf16), jax.ShapeDtypeStruct((PLANE, HD, FINE + HD), bf16)),
        [VMEM] * 3,
        0,
        9 * 2**19,
        out_specs=(VMEM, VMEM),
    )(got, w_out, rotation[0, 0])
    pair_other = z_swap(pair_own)
    wo_ring = exchange(wo_pack, ("x", "y"))
    queries = got[:, :, :HD]

    mixed = on_core(
        attend_body,
        jax.ShapeDtypeStruct((PLANE, TOK + ROWS * TILES, HD), bf16),
        [SMEM] + [VMEM] * 8 + [HELD],
        10**8,
        3 * 2**20,
    )(spot, queries, pair_own, pair_other, cosine, sine, down, across, goal, wo_ring)
    mixed = exchange(mixed, ("x", "y"))

    wide_slice = jax.ShapeDtypeStruct((TOK, FINE), f32)
    terms, terms_sent, goal_slice = on_core(
        terms_body,
        (wide_slice, jax.ShapeDtypeStruct((TOK, FINE), bf16), wide_slice),
        [SMEM, VMEM, VMEM],
        2 * TOK * PLANE * HD * (FINE + HD),
        4 * 2**20,
        out_specs=(VMEM,) * 3,
    )(spot, mixed, wo_ring)
    terms_other = z_swap(terms_sent)

    parts = on_core(
        grads_body,
        jax.ShapeDtypeStruct((PLANE, HD + ROWS * TILES, HD), bf16),
        [SMEM] + [VMEM] * 6,
        2 * TOK * PLANE * HD * (FINE + HD),
        6 * 2**20,
        [pltpu.VMEM((TOK, FINE), f32)],
    )(spot, terms, terms_other, raw, goal_slice, mixed, wo_ring)
    parts = exchange(parts, ("x", "y"))

    out_rows, rot_grad = on_core(
        finish_body,
        (jax.ShapeDtypeStruct((ROWS, D), bf16), jax.ShapeDtypeStruct((HD, HD), f32)),
        [VMEM],
        10**6,
        2**20,
        out_specs=(VMEM, VMEM),
    )(parts)
    return (out_rows[None], rot_grad[None, None])


def solution(mesh):
    devices = mesh.devices
    grid = Mesh(devices.reshape(devices.shape[0], NX, NY, NZ), EVERY)
    head = ("x", "y", "z")
    in_specs = (
        P("phase", head, None),
        P("phase", None),
        P("phase", None),
        P("phase", None, head),
        P("phase", None, head),
        P("phase", head, None, None),
        P("phase", head, None),
        P("phase", head, None),
    )
    out_specs = (P("phase", head, None), P("phase", head, None, None))
    return jax.shard_map(local, mesh=grid, in_specs=in_specs, out_specs=out_specs, check_vma=False)
```

```python
import jax
import jax.numpy as jnp
from jax import lax
from jax.experimental import pallas as pl
from jax.experimental.pallas import tpu as pltpu
from jax.sharding import Mesh, PartitionSpec as P

HD = 128
NX, NY, NZ = 4, 4, 2
PLANE = NX * NY
PIECE = 32
TOK = 256
ROWS = 8
D = 8192
PART = D // NY
FINE = D // PLANE
TILES = FINE // HD
bf16 = jnp.bfloat16
f32 = jnp.float32
rope_base = 500000.0
masked_score = -1e30
EVERY = ("phase", "x", "y", "z")
VMEM = pl.BlockSpec(memory_space=pltpu.VMEM)
SMEM = pl.BlockSpec(memory_space=pltpu.SMEM)
HELD = pl.BlockSpec(memory_space=pl.ANY)


def on_core(body, out_shape, in_specs, flops, moved, scratch=(), out_specs=VMEM):
    return pl.pallas_call(
        body,
        out_shape=out_shape,
        in_specs=in_specs,
        out_specs=out_specs,
        scratch_shapes=list(scratch),
        compiler_params=pltpu.CompilerParams(vmem_limit_bytes=40 * 2**20),
        cost_estimate=pl.CostEstimate(flops=flops, bytes_accessed=moved, transcendentals=0),
    )


def dot(a, b, dims=((1,), (0,))):
    return lax.dot_general(a, b, (dims, ((), ())), preferred_element_type=f32)


def relay(block, flip):
    phases = lax.axis_size("phase")
    heads = PLANE * NZ
    pairs = [
        (p * heads + h, (p + 1) % phases * heads + (h ^ flip)) for p in range(phases) for h in range(heads)
    ]
    return lax.ppermute(block, EVERY, pairs)


def z_swap(block):
    return lax.ppermute(block, "z", [(0, 1), (1, 0)])


def exchange(blocks, axes):
    return lax.all_to_all(blocks, axes, 0, 0, tiled=True)


def fine_column(place):
    return place % NY * PART + place // NY * FINE


def fold(rows):
    return jnp.concatenate([rows[:, k * HD : (k + 1) * HD] for k in range(TILES)], axis=0)


def unfold(rows):
    return jnp.concatenate([rows[k * ROWS : (k + 1) * ROWS] for k in range(TILES)], axis=1)


def pack_in_body(wq_ref, wkv_ref, out_ref):
    for y in range(NY):
        start = y * PART
        out_ref[y, :PART] = wq_ref[start : start + PART]
        for k in range(PART // HD):
            first = PART + k * PIECE
            out_ref[y, first : first + PIECE] = wkv_ref[:, start + k * HD : start + (k + 1) * HD]


def pack_out_body(got_ref, w_ref, tables_ref, query_ref, pair_ref, out_ref):
    total = got_ref[0].astype(f32)
    for y in range(1, NY):
        total = total + got_ref[y].astype(f32)
    query_ref[...] = rotate(total[:, :HD], tables_ref[0], tables_ref[1]).astype(bf16)
    pair_ref[...] = rotate(total[:, HD:], tables_ref[2], tables_ref[3]).astype(bf16)
    for place in range(PLANE):
        start = fine_column(place)
        out_ref[place] = w_ref[:, start : start + FINE]


def pack_rows_body(spot_ref, own_ref, other_ref, goal_ref, *refs):
    out_ref, kept_ref = refs[-2:]
    kept_ref[...] = goal_ref[...]
    own = own_ref[...].astype(f32)
    other = other_ref[...].astype(f32)
    at_zero = spot_ref[2] == 0
    wide = jnp.concatenate([jnp.where(at_zero, own, other), jnp.where(at_zero, other, own)], axis=0)
    scale = lax.rsqrt(jnp.mean(wide * wide, axis=-1, keepdims=True) + 1e-05)
    high = scale.astype(bf16).astype(f32)
    lane = lax.broadcasted_iota(jnp.int32, (2 * ROWS, HD), 1)
    tail = jnp.where(lane < HD // 2, high, scale - high).astype(bf16)
    narrow = wide.astype(bf16)
    for place in range(PLANE):
        y = place % NY
        out_ref[place, :, :PART] = narrow[:, y * PART : (y + 1) * PART]
        out_ref[place, :, PART:] = tail


def project_body(spot_ref, x_ref, gain_ref, ring_ref, out_ref, raw_ref, pair_ref):
    raw_ref[...] = x_ref[:, pl.ds(pl.multiple_of(spot_ref[0] * FINE, FINE), FINE)]
    tail = x_ref[:, PART:].astype(f32)
    scale = tail[:, 0:1] + tail[:, HD // 2 : HD // 2 + 1]
    normed = (x_ref[:, :PART].astype(f32) * scale * gain_ref[...].astype(f32)).astype(bf16)
    for y in range(NY):
        for k in range(PART // HD):
            first = PART + k * PIECE
            pair_ref[y * PIECE : (y + 1) * PIECE, k * HD : (k + 1) * HD] = ring_ref[y, first : first + PIECE]
    pair = dot(normed, pair_ref[...], ((1,), (1,))).astype(bf16)
    for y in range(NY):
        out_ref[y, :, :HD] = dot(normed, ring_ref[y, :PART]).astype(bf16)
        out_ref[y, :, HD:] = pair


def rotate(values, cosine, signed_sine):
    lane = lax.broadcasted_iota(jnp.int32, values.shape, 1)
    swapped = jnp.where(lane % 2 == 0, jnp.roll(values, -1, axis=1), jnp.roll(values, 1, axis=1))
    return values * cosine + swapped * signed_sine


def attend_body(spot_ref, query_at, own_at, other_at, across_ref, turn_ref, held_ref, out_ref, mixed_ref, held, sems):
    copies = [pltpu.make_async_copy(at, held.at[i], sems.at[i]) for i, at in enumerate((query_at, own_at, other_at))]
    for copy in copies:
        copy.start()
    order = lax.broadcasted_iota(jnp.int32, (TOK, TOK), 0)
    against = lax.broadcasted_iota(jnp.int32, (TOK, TOK), 1)
    across = across_ref[...].astype(f32)
    down = jnp.sum(jnp.where(order == against, across, 0.0), axis=1, keepdims=True)
    allowed = (down == across) & (against <= order)
    for copy in copies:
        copy.wait()
    query = held[0]
    own = held[1].astype(f32)
    other = held[2].astype(f32)
    at_zero = spot_ref[2] == 0
    even = jnp.where(at_zero, own, other)
    odd = jnp.where(at_zero, other, own)
    quarter = lax.broadcasted_iota(jnp.int32, (TOK, HD), 1) // PIECE

    def weave(a, b, c, d):
        return jnp.where(quarter == 0, a, jnp.where(quarter == 1, b, jnp.where(quarter == 2, c, d)))

    def turn(values, by):
        return jnp.roll(values, by * PIECE, axis=1)

    key_block = weave(even, turn(odd, 1), turn(even, 1), turn(odd, 2)).astype(bf16)
    value_block = weave(turn(even, 2), turn(odd, 3), turn(even, 3), odd).astype(bf16)
    scores = dot(query, key_block, ((1,), (1,))) * HD ** (-0.5)
    scores = jnp.where(allowed, scores, masked_score)
    peak = jnp.max(scores, axis=1, keepdims=True)
    powers = jnp.where(allowed, jnp.exp(scores - peak), 0.0)
    prob = (powers / jnp.sum(powers, axis=1, keepdims=True)).astype(bf16)
    mixed = dot(prob, value_block).astype(bf16)
    mixed_ref[...] = mixed
    turned = dot(mixed, turn_ref[...]).astype(bf16)
    for place in range(PLANE):
        out_ref[place] = turned


def pack_goal_body(spot_ref, own_ref, other_ref, out_ref):
    own = own_ref[...].astype(f32)
    other = other_ref[...].astype(f32)
    at_zero = spot_ref[2] == 0
    goal = jnp.concatenate([jnp.where(at_zero, own, other), jnp.where(at_zero, other, own)], axis=0).astype(bf16)
    for place in range(PLANE):
        start = fine_column(place)
        for k in range(TILES):
            out_ref[place, 16 * k : 16 * k + 16] = goal[:, start + k * HD : start + (k + 1) * HD]


def terms_body(got_ref, w_ref, mixed_ref, goal_ref, out_ref, sent_ref, pack_ref):
    total = jnp.zeros((TOK, FINE), f32)
    mixed = mixed_ref[...]
    for place in range(0, PLANE, 2):
        turned = jnp.concatenate([got_ref[place], got_ref[place + 1]], axis=1)
        weights = jnp.concatenate([w_ref[place], w_ref[place + 1]], axis=0)
        total = total + dot(turned, weights)
        for h in (place, place + 1):
            pack_ref[h, :TOK] = mixed
            pack_ref[h, TOK:] = goal_ref[h]
    out_ref[...] = total
    sent_ref[...] = total.astype(bf16)


def grads_body(spot_ref, own_ref, other_ref, x_ref, got_ref, w_ref, out_ref, wide_ref):
    passed = x_ref[...].astype(f32) + (own_ref[...] + other_ref[...].astype(f32))
    wide = passed.astype(bf16).astype(f32)
    wide_ref[...] = wide
    rows = [
        jnp.concatenate([got_ref[place, TOK + 16 * k : TOK + 16 * k + 16] for k in range(TILES)], axis=1)
        for place in range(PLANE)
    ]
    error = (wide - jnp.concatenate(rows, axis=0).astype(f32)).astype(bf16)
    for place in range(0, PLANE, 2):
        pair = (place, place + 1)
        weights = jnp.concatenate([w_ref[h] for h in pair], axis=0)
        back = dot(error, weights, ((1,), (1,))).astype(bf16)
        for i, h in enumerate(pair):
            part = dot(got_ref[h, :TOK], back[:, i * HD : (i + 1) * HD], ((0,), (0,)))
            out_ref[h, :HD] = part.astype(bf16)
    for place in range(PLANE):
        first = pl.multiple_of(place * 2 * ROWS + spot_ref[2] * ROWS, ROWS)
        out_ref[place, HD:] = fold(wide_ref[pl.ds(first, ROWS), :]).astype(bf16)


def finish_body(got_ref, rows_ref, grad_ref):
    total = got_ref[0, :HD].astype(f32)
    for place in range(1, PLANE):
        total = total + got_ref[place, :HD].astype(f32)
    grad_ref[...] = total
    for place in range(PLANE):
        start = fine_column(place)
        rows_ref[:, start : start + FINE] = unfold(got_ref[place, HD:].astype(f32)).astype(bf16)


def tables(segments, z_at):
    order = jnp.arange(TOK, dtype=jnp.int32)
    same = segments[:, None] == segments[None, :]
    earlier = order[None, :] < order[:, None]
    positions = jnp.sum((same & earlier).astype(jnp.int32), axis=1).astype(f32)
    lane = jnp.arange(HD, dtype=jnp.int32)
    column = lane // PIECE * (NZ * PIECE) + z_at * PIECE + lane % PIECE
    column = jnp.stack([lane, jnp.where(lane < 2 * PIECE, column, 0)])
    turns = jnp.stack([lane >= 0, lane < 2 * PIECE])
    freq = jnp.where(turns, jnp.power(rope_base, -(2.0 * (column // 2).astype(f32)) / HD), 0.0)
    angle = positions[None, :, None] * freq[:, None, :]
    sine = jnp.sin(angle)
    signed = jnp.where(lane[None, None, :] % 2 == 0, -sine, sine)
    both = jnp.stack([jnp.cos(angle), signed], axis=1)
    return both.reshape(4, TOK, HD)


def local(handoff, segment_ids, norm_gain, query_weight, kv_weight, rotation, out_weight, target):
    segments = segment_ids[0]
    w_query = query_weight[0]
    w_pair = kv_weight[0].T
    w_out = out_weight[0]
    x_at, y_at, z_at = lax.axis_index("x"), lax.axis_index("y"), lax.axis_index("z")
    spot = jnp.stack([x_at, y_at, z_at]).astype(jnp.int32)
    gain = lax.dynamic_slice_in_dim(norm_gain, y_at * PART, PART, 1)
    turning = tables(segments, z_at)


    own, other = relay(handoff[0], 0), relay(handoff[0], 1)
    depth = PART + PART * PIECE // HD
    rings = on_core(
        pack_in_body,
        jax.ShapeDtypeStruct((NY, depth, HD), bf16),
        [VMEM, VMEM],
        0,
        5 * 2**20,
    )(w_query, w_pair)
    rings = exchange(rings, "y")

    rows, goal = on_core(
        pack_rows_body,
        (
            jax.ShapeDtypeStruct((PLANE, 2 * ROWS, PART + HD), bf16),
            jax.ShapeDtypeStruct((ROWS, D), bf16),
        ),
        [SMEM, VMEM, VMEM, VMEM] + [HELD] * 2,
        10**6,
        3 * 2**20,
        out_specs=(VMEM, VMEM),
    )(spot, own, other, target[0], rings, turning)
    goal_other = z_swap(goal)
    features = exchange(rows, ("x", "y")).reshape(TOK, PART + HD)

    sent, raw = on_core(
        project_body,
        (jax.ShapeDtypeStruct((NY, TOK, 2 * HD), bf16), jax.ShapeDtypeStruct((TOK, FINE), bf16)),
        [SMEM] + [VMEM] * 3,
        2 * TOK * PART * 5 * HD,
        5 * 2**20,
        [pltpu.VMEM((HD, PART), bf16)],
        out_specs=(VMEM, VMEM),
    )(spot, features, gain, rings)
    got = exchange(sent, "y")

    narrow = jax.ShapeDtypeStruct((TOK, HD), bf16)
    query, pair_own, wo_pack = on_core(
        pack_out_body,
        (narrow, narrow, jax.ShapeDtypeStruct((PLANE, HD, FINE), bf16)),
        [VMEM] * 3,
        0,
        4 * 2**20,
        out_specs=(VMEM,) * 3,
    )(got, w_out, turning)
    pair_other = z_swap(pair_own)
    wo_ring = exchange(wo_pack, ("x", "y"))

    turned, mixed = on_core(
        attend_body,
        (jax.ShapeDtypeStruct((PLANE, TOK, HD), bf16), narrow),
        [SMEM] + [HELD] * 3 + [VMEM] * 2 + [HELD],
        10**8,
        3 * 2**20,
        [pltpu.VMEM((3, TOK, HD), bf16), pltpu.SemaphoreType.DMA((3,))],
        out_specs=(VMEM, VMEM),
    )(spot, query, pair_own, pair_other, segments[None, :], rotation[0, 0], wo_ring)
    goal_pack = on_core(
        pack_goal_body,
        jax.ShapeDtypeStruct((PLANE, 2 * ROWS * TILES, HD), bf16),
        [SMEM, VMEM, VMEM],
        10**6,
        2**19,
    )(spot, goal, goal_other)
    turned = exchange(turned, ("x", "y"))

    terms, terms_sent, mixed_pack = on_core(
        terms_body,
        (
            jax.ShapeDtypeStruct((TOK, FINE), f32),
            jax.ShapeDtypeStruct((TOK, FINE), bf16),
            jax.ShapeDtypeStruct((PLANE, TOK + 2 * ROWS * TILES, HD), bf16),
        ),
        [VMEM] * 4,
        2 * TOK * PLANE * HD * FINE,
        4 * 2**20,
        out_specs=(VMEM,) * 3,
    )(turned, wo_ring, mixed, goal_pack)
    terms_other = z_swap(terms_sent)
    mixed_ring = exchange(mixed_pack, ("x", "y"))

    parts = on_core(
        grads_body,
        jax.ShapeDtypeStruct((PLANE, HD + ROWS * TILES, HD), bf16),
        [SMEM] + [VMEM] * 5,
        2 * TOK * PLANE * HD * (FINE + HD),
        6 * 2**20,
        [pltpu.VMEM((TOK, FINE), f32)],
    )(spot, terms, terms_other, raw, mixed_ring, wo_ring)
    parts = exchange(parts, ("x", "y"))

    out_rows, rot_grad = on_core(
        finish_body,
        (jax.ShapeDtypeStruct((ROWS, D), bf16), jax.ShapeDtypeStruct((HD, HD), f32)),
        [VMEM],
        10**6,
        2**20,
        out_specs=(VMEM, VMEM),
    )(parts)
    return (out_rows[None], rot_grad[None, None])


def solution(mesh):
    devices = mesh.devices
    grid = Mesh(devices.reshape(devices.shape[0], NX, NY, NZ), EVERY)
    head = ("x", "y", "z")
    in_specs = (
        P("phase", head, None),
        P("phase", None),
        P("phase", None),
        P("phase", None, head),
        P("phase", None, head),
        P("phase", head, None, None),
        P("phase", head, None),
        P("phase", head, None),
    )
    out_specs = (P("phase", head, None), P("phase", head, None, None))
    return jax.shard_map(local, mesh=grid, in_specs=in_specs, out_specs=out_specs, check_vma=False)
```

```python
import jax
import jax.numpy as jnp
from jax import lax
from jax.experimental import pallas as pl
from jax.experimental.pallas import tpu as pltpu
from jax.sharding import Mesh, PartitionSpec as P

HD = 128
NX, NY, NZ = 4, 4, 2
PLANE = NX * NY
PIECE = 32
TOK = 256
ROWS = 8
D = 8192
PART = D // NY
FINE = D // PLANE
TILES = FINE // HD
bf16 = jnp.bfloat16
f32 = jnp.float32
rope_base = 500000.0
masked_score = -1e30
EVERY = ("phase", "x", "y", "z")
VMEM = pl.BlockSpec(memory_space=pltpu.VMEM)
SMEM = pl.BlockSpec(memory_space=pltpu.SMEM)
HELD = pl.BlockSpec(memory_space=pl.ANY)


def on_core(body, out_shape, in_specs, flops, moved, scratch=(), out_specs=VMEM, aliases=None):
    return pl.pallas_call(
        body,
        out_shape=out_shape,
        in_specs=in_specs,
        out_specs=out_specs,
        scratch_shapes=list(scratch),
        input_output_aliases=aliases or {},
        compiler_params=pltpu.CompilerParams(vmem_limit_bytes=40 * 2**20),
        cost_estimate=pl.CostEstimate(flops=flops, bytes_accessed=moved, transcendentals=0),
    )


def dot(a, b, dims=((1,), (0,))):
    return lax.dot_general(a, b, (dims, ((), ())), preferred_element_type=f32)


def relay(block, flip):
    phases = lax.axis_size("phase")
    heads = PLANE * NZ
    pairs = [
        (p * heads + h, (p + 1) % phases * heads + (h ^ flip)) for p in range(phases) for h in range(heads)
    ]
    return lax.ppermute(block, EVERY, pairs)


def z_swap(block):
    return lax.ppermute(block, "z", [(0, 1), (1, 0)])


def exchange(blocks, axes):
    return lax.all_to_all(blocks, axes, 0, 0, tiled=True)


def fine_column(place):
    return place % NY * PART + place // NY * FINE


def fold(rows):
    return jnp.concatenate([rows[:, k * HD : (k + 1) * HD] for k in range(TILES)], axis=0)


def unfold(rows):
    return jnp.concatenate([rows[k * ROWS : (k + 1) * ROWS] for k in range(TILES)], axis=1)


def carry_out(copies):
    for copy in copies:
        copy.start()
    for copy in copies:
        copy.wait()


def pack_in_body(wq_at, wkv_at, out_at, sems):
    copies = []
    for y in range(NY):
        start = y * PART
        copies.append((wq_at.at[start : start + PART], out_at.at[y, :PART]))
        for k in range(PART // HD):
            first = PART + k * PIECE
            copies.append((wkv_at.at[:, start + k * HD : start + (k + 1) * HD], out_at.at[y, first : first + PIECE]))
    carry_out([pltpu.make_async_copy(a, b, sems.at[i]) for i, (a, b) in enumerate(copies)])


def pack_out_body(w_at, turn_at, out_at, sems):
    copies = []
    for place in range(PLANE):
        start = fine_column(place)
        copies.append((w_at.at[:, start : start + FINE], out_at.at[place, :, :FINE]))
        copies.append((turn_at, out_at.at[place, :, FINE:]))
    carry_out([pltpu.make_async_copy(a, b, sems.at[i]) for i, (a, b) in enumerate(copies)])


def gather_body(got_ref, tables_ref, pack_at, query_ref, pair_ref, same_at):
    total = got_ref[0].astype(f32)
    for y in range(1, NY):
        total = total + got_ref[y].astype(f32)
    query_ref[...] = rotate(total[:, :HD], tables_ref[0], tables_ref[1]).astype(bf16)
    pair_ref[...] = rotate(total[:, HD:], tables_ref[2], tables_ref[3]).astype(bf16)


def pack_rows_body(spot_ref, own_ref, other_ref, *refs):
    out_ref = refs[-1]
    own = own_ref[...].astype(f32)
    other = other_ref[...].astype(f32)
    at_zero = spot_ref[2] == 0
    wide = jnp.concatenate([jnp.where(at_zero, own, other), jnp.where(at_zero, other, own)], axis=0)
    scale = lax.rsqrt(jnp.mean(wide * wide, axis=-1, keepdims=True) + 1e-05)
    high = scale.astype(bf16).astype(f32)
    lane = lax.broadcasted_iota(jnp.int32, (2 * ROWS, HD), 1)
    tail = jnp.where(lane < HD // 2, high, scale - high).astype(bf16)
    narrow = wide.astype(bf16)
    for place in range(PLANE):
        y = place % NY
        out_ref[place, :, :PART] = narrow[:, y * PART : (y + 1) * PART]
        out_ref[place, :, PART:] = tail


def project_body(spot_ref, x_ref, gain_ref, ring_ref, out_ref, raw_ref, pair_ref):
    raw_ref[...] = x_ref[:, pl.ds(pl.multiple_of(spot_ref[0] * FINE, FINE), FINE)]
    tail = x_ref[:, PART:].astype(f32)
    scale = tail[:, 0:1] + tail[:, HD // 2 : HD // 2 + 1]
    normed = (x_ref[:, :PART].astype(f32) * scale * gain_ref[...].astype(f32)).astype(bf16)
    for y in range(NY):
        for k in range(PART // HD):
            first = PART + k * PIECE
            pair_ref[y * PIECE : (y + 1) * PIECE, k * HD : (k + 1) * HD] = ring_ref[y, first : first + PIECE]
    pair = dot(normed, pair_ref[...], ((1,), (1,))).astype(bf16)
    for y in range(NY):
        out_ref[y, :, :HD] = dot(normed, ring_ref[y, :PART]).astype(bf16)
        out_ref[y, :, HD:] = pair


def rotate(values, cosine, signed_sine):
    lane = lax.broadcasted_iota(jnp.int32, values.shape, 1)
    swapped = jnp.where(lane % 2 == 0, jnp.roll(values, -1, axis=1), jnp.roll(values, 1, axis=1))
    return values * cosine + swapped * signed_sine


def attend_body(spot_ref, query_at, own_at, other_at, across_ref, goal_ref, held_ref, out_ref, held, sems):
    copies = [pltpu.make_async_copy(at, held.at[i], sems.at[i]) for i, at in enumerate((query_at, own_at, other_at))]
    for copy in copies:
        copy.start()
    order = lax.broadcasted_iota(jnp.int32, (TOK, TOK), 0)
    against = lax.broadcasted_iota(jnp.int32, (TOK, TOK), 1)
    across = across_ref[...].astype(f32)
    down = jnp.sum(jnp.where(order == against, across, 0.0), axis=1, keepdims=True)
    allowed = (down == across) & (against <= order)
    for copy in copies:
        copy.wait()
    query = held[0]
    own = held[1].astype(f32)
    other = held[2].astype(f32)
    at_zero = spot_ref[2] == 0
    even = jnp.where(at_zero, own, other)
    odd = jnp.where(at_zero, other, own)
    quarter = lax.broadcasted_iota(jnp.int32, (TOK, HD), 1) // PIECE

    def weave(a, b, c, d):
        return jnp.where(quarter == 0, a, jnp.where(quarter == 1, b, jnp.where(quarter == 2, c, d)))

    def turn(values, by):
        return jnp.roll(values, by * PIECE, axis=1)

    key_block = weave(even, turn(odd, 1), turn(even, 1), turn(odd, 2)).astype(bf16)
    value_block = weave(turn(even, 2), turn(odd, 3), turn(even, 3), odd).astype(bf16)
    scores = dot(query, key_block, ((1,), (1,))) * HD ** (-0.5)
    scores = jnp.where(allowed, scores, masked_score)
    peak = jnp.max(scores, axis=1, keepdims=True)
    powers = jnp.where(allowed, jnp.exp(scores - peak), 0.0)
    prob = (powers / jnp.sum(powers, axis=1, keepdims=True)).astype(bf16)
    mixed = dot(prob, value_block).astype(bf16)
    goal = goal_ref[...].astype(f32)
    for place in range(PLANE):
        start = fine_column(place)
        out_ref[place, :TOK] = mixed
        out_ref[place, TOK:] = fold(goal[:, start : start + FINE]).astype(bf16)


def terms_body(spot_ref, got_ref, w_ref, out_ref, sent_ref, goal_ref):
    goal_ref[...] = jnp.zeros((TOK, FINE), f32)
    total = jnp.zeros((TOK, FINE), f32)
    for place in range(PLANE):
        first = pl.multiple_of(place * 2 * ROWS + spot_ref[2] * ROWS, ROWS)
        goal_ref[pl.ds(first, ROWS), :] = unfold(got_ref[place, TOK:].astype(f32))
    for place in range(0, PLANE, 2):
        pair = (place, place + 1)
        turned = [dot(got_ref[h, :TOK], w_ref[h, :, FINE:]).astype(bf16) for h in pair]
        weights = jnp.concatenate([w_ref[h, :, :FINE] for h in pair], axis=0)
        total = total + dot(jnp.concatenate(turned, axis=1), weights)
    out_ref[...] = total
    sent_ref[...] = (total - goal_ref[...]).astype(bf16)


def grads_body(spot_ref, own_ref, other_ref, x_ref, goal_ref, got_ref, w_ref, out_ref, wide_ref):
    passed = x_ref[...].astype(f32) + (own_ref[...] + other_ref[...].astype(f32))
    wide = passed.astype(bf16).astype(f32)
    wide_ref[...] = wide
    error = (wide - goal_ref[...]).astype(bf16)
    for place in range(0, PLANE, 2):
        pair = (place, place + 1)
        weights = jnp.concatenate([w_ref[h, :, :FINE] for h in pair], axis=0)
        back = dot(error, weights, ((1,), (1,))).astype(bf16)
        for i, h in enumerate(pair):
            part = dot(got_ref[h, :TOK], back[:, i * HD : (i + 1) * HD], ((0,), (0,)))
            out_ref[h, :HD] = part.astype(bf16)
    for place in range(PLANE):
        first = pl.multiple_of(place * 2 * ROWS + spot_ref[2] * ROWS, ROWS)
        out_ref[place, HD:] = fold(wide_ref[pl.ds(first, ROWS), :]).astype(bf16)


def finish_body(got_ref, rows_ref, grad_ref):
    total = got_ref[0, :HD].astype(f32)
    for place in range(1, PLANE):
        total = total + got_ref[place, :HD].astype(f32)
    grad_ref[...] = total
    for place in range(PLANE):
        start = fine_column(place)
        rows_ref[:, start : start + FINE] = unfold(got_ref[place, HD:].astype(f32)).astype(bf16)


def tables(segments, z_at):
    order = jnp.arange(TOK, dtype=jnp.int32)
    same = segments[:, None] == segments[None, :]
    earlier = order[None, :] < order[:, None]
    positions = jnp.sum((same & earlier).astype(jnp.int32), axis=1).astype(f32)
    lane = jnp.arange(HD, dtype=jnp.int32)
    column = lane // PIECE * (NZ * PIECE) + z_at * PIECE + lane % PIECE
    column = jnp.stack([lane, jnp.where(lane < 2 * PIECE, column, 0)])
    turns = jnp.stack([lane >= 0, lane < 2 * PIECE])
    freq = jnp.where(turns, jnp.power(rope_base, -(2.0 * (column // 2).astype(f32)) / HD), 0.0)
    angle = positions[None, :, None] * freq[:, None, :]
    sine = jnp.sin(angle)
    signed = jnp.where(lane[None, None, :] % 2 == 0, -sine, sine)
    both = jnp.stack([jnp.cos(angle), signed], axis=1)
    return both.reshape(4, TOK, HD)


def local(handoff, segment_ids, norm_gain, query_weight, kv_weight, rotation, out_weight, target):
    segments = segment_ids[0]
    w_query = query_weight[0]
    w_pair = kv_weight[0].T
    w_out = out_weight[0]
    goal = target[0]
    x_at, y_at, z_at = lax.axis_index("x"), lax.axis_index("y"), lax.axis_index("z")
    spot = jnp.stack([x_at, y_at, z_at]).astype(jnp.int32)
    gain = lax.dynamic_slice_in_dim(norm_gain, y_at * PART, PART, 1)
    turning = tables(segments, z_at)

    own, other = relay(handoff[0], 0), relay(handoff[0], 1)
    depth = PART + PART * PIECE // HD
    rings = on_core(
        pack_in_body,
        jax.ShapeDtypeStruct((NY, depth, HD), bf16),
        [HELD, HELD],
        0,
        5 * 2**20,
        [pltpu.SemaphoreType.DMA((NY + D // HD,))],
        out_specs=HELD,
    )(w_query, w_pair)
    wo_pack = on_core(
        pack_out_body,
        jax.ShapeDtypeStruct((PLANE, HD, FINE + HD), bf16),
        [HELD, HELD],
        0,
        5 * 2**20,
        [pltpu.SemaphoreType.DMA((2 * PLANE,))],
        out_specs=HELD,
    )(w_out, rotation[0, 0])
    rings = exchange(rings, "y")

    rows = on_core(
        pack_rows_body,
        jax.ShapeDtypeStruct((PLANE, 2 * ROWS, PART + HD), bf16),
        [SMEM, VMEM, VMEM] + [HELD] * 4,
        10**6,
        3 * 2**20,
    )(spot, own, other, rings, turning, wo_pack, gain)
    features = exchange(rows, ("x", "y")).reshape(TOK, PART + HD)

    sent, raw = on_core(
        project_body,
        (jax.ShapeDtypeStruct((NY, TOK, 2 * HD), bf16), jax.ShapeDtypeStruct((TOK, FINE), bf16)),
        [SMEM] + [VMEM] * 3,
        2 * TOK * PART * 5 * HD,
        5 * 2**20,
        [pltpu.VMEM((HD, PART), bf16)],
        out_specs=(VMEM, VMEM),
    )(spot, features, gain, rings)
    got = exchange(sent, "y")

    narrow = jax.ShapeDtypeStruct((TOK, HD), bf16)
    query, pair_own, wo_pack = on_core(
        gather_body,
        (narrow, narrow, jax.ShapeDtypeStruct(wo_pack.shape, bf16)),
        [VMEM, VMEM, HELD],
        10**6,
        2**20,
        out_specs=(VMEM, VMEM, HELD),
        aliases={2: 2},
    )(got, turning, wo_pack)
    pair_other = z_swap(pair_own)
    wo_ring = exchange(wo_pack, ("x", "y"))

    mixed = on_core(
        attend_body,
        jax.ShapeDtypeStruct((PLANE, TOK + ROWS * TILES, HD), bf16),
        [SMEM] + [HELD] * 3 + [VMEM] * 2 + [HELD],
        10**8,
        3 * 2**20,
        [pltpu.VMEM((3, TOK, HD), bf16), pltpu.SemaphoreType.DMA((3,))],
    )(spot, query, pair_own, pair_other, segments[None, :], goal, wo_ring)
    mixed = exchange(mixed, ("x", "y"))

    wide_slice = jax.ShapeDtypeStruct((TOK, FINE), f32)
    terms, terms_sent, goal_slice = on_core(
        terms_body,
        (wide_slice, jax.ShapeDtypeStruct((TOK, FINE), bf16), wide_slice),
        [SMEM, VMEM, VMEM],
        2 * TOK * PLANE * HD * (FINE + HD),
        4 * 2**20,
        out_specs=(VMEM,) * 3,
    )(spot, mixed, wo_ring)
    terms_other = z_swap(terms_sent)

    parts = on_core(
        grads_body,
        jax.ShapeDtypeStruct((PLANE, HD + ROWS * TILES, HD), bf16),
        [SMEM] + [VMEM] * 6,
        2 * TOK * PLANE * HD * (FINE + HD),
        6 * 2**20,
        [pltpu.VMEM((TOK, FINE), f32)],
    )(spot, terms, terms_other, raw, goal_slice, mixed, wo_ring)
    parts = exchange(parts, ("x", "y"))

    out_rows, rot_grad = on_core(
        finish_body,
        (jax.ShapeDtypeStruct((ROWS, D), bf16), jax.ShapeDtypeStruct((HD, HD), f32)),
        [VMEM],
        10**6,
        2**20,
        out_specs=(VMEM, VMEM),
    )(parts)
    return (out_rows[None], rot_grad[None, None])


def solution(mesh):
    devices = mesh.devices
    grid = Mesh(devices.reshape(devices.shape[0], NX, NY, NZ), EVERY)
    head = ("x", "y", "z")
    in_specs = (
        P("phase", head, None),
        P("phase", None),
        P("phase", None),
        P("phase", None, head),
        P("phase", None, head),
        P("phase", head, None, None),
        P("phase", head, None),
        P("phase", head, None),
    )
    out_specs = (P("phase", head, None), P("phase", head, None, None))
    return jax.shard_map(local, mesh=grid, in_specs=in_specs, out_specs=out_specs, check_vma=False)
```

```python
import jax
import jax.numpy as jnp
from jax import lax
from jax.experimental import pallas as pl
from jax.experimental.pallas import tpu as pltpu
from jax.sharding import Mesh, PartitionSpec as P

HD = 128
NX, NY, NZ = 4, 4, 2
PLANE = NX * NY
PIECE = 32
TOK = 256
ROWS = 8
D = 8192
PART = D // NY
FINE = D // PLANE
TILES = FINE // HD
bf16 = jnp.bfloat16
f32 = jnp.float32
rope_base = 500000.0
masked_score = -1e30
EVERY = ("phase", "x", "y", "z")
VMEM = pl.BlockSpec(memory_space=pltpu.VMEM)
SMEM = pl.BlockSpec(memory_space=pltpu.SMEM)
HELD = pl.BlockSpec(memory_space=pl.ANY)


def on_core(body, out_shape, in_specs, flops, moved, scratch=(), out_specs=VMEM, aliases=None, room=40):
    return pl.pallas_call(
        body,
        out_shape=out_shape,
        in_specs=in_specs,
        out_specs=out_specs,
        scratch_shapes=list(scratch),
        input_output_aliases=aliases or {},
        compiler_params=pltpu.CompilerParams(vmem_limit_bytes=room * 2**20),
        cost_estimate=pl.CostEstimate(flops=flops, bytes_accessed=moved, transcendentals=0),
    )


def dot(a, b, dims=((1,), (0,))):
    return lax.dot_general(a, b, (dims, ((), ())), preferred_element_type=f32)


def relay(block, flip):
    phases = lax.axis_size("phase")
    heads = PLANE * NZ
    pairs = [
        (p * heads + h, (p + 1) % phases * heads + (h ^ flip)) for p in range(phases) for h in range(heads)
    ]
    return lax.ppermute(block, EVERY, pairs)


def z_swap(block):
    return lax.ppermute(block, "z", [(0, 1), (1, 0)])


def exchange(blocks, axes):
    return lax.all_to_all(blocks, axes, 0, 0, tiled=True)


def fine_column(place):
    return place % NY * PART + place // NY * FINE


def fold(rows):
    return jnp.concatenate([rows[:, k * HD : (k + 1) * HD] for k in range(TILES)], axis=0)


def unfold(rows):
    return jnp.concatenate([rows[k * ROWS : (k + 1) * ROWS] for k in range(TILES)], axis=1)


def carry_out(copies):
    for copy in copies:
        copy.start()
    for copy in copies:
        copy.wait()


def pack_in_body(wq_at, wkv_at, out_at, sems):
    copies = []
    for y in range(NY):
        start = y * PART
        copies.append((wq_at.at[start : start + PART], out_at.at[y, :PART]))
        for k in range(PART // HD):
            first = PART + k * PIECE
            copies.append((wkv_at.at[:, start + k * HD : start + (k + 1) * HD], out_at.at[y, first : first + PIECE]))
    carry_out([pltpu.make_async_copy(a, b, sems.at[i]) for i, (a, b) in enumerate(copies)])


def pack_out_body(w_at, turn_at, out_at, sems):
    copies = []
    for place in range(PLANE):
        start = fine_column(place)
        copies.append((w_at.at[:, start : start + FINE], out_at.at[place, :, :FINE]))
        copies.append((turn_at, out_at.at[place, :, FINE:]))
    carry_out([pltpu.make_async_copy(a, b, sems.at[i]) for i, (a, b) in enumerate(copies)])


def gather_body(got_ref, tables_ref, pack_at, query_ref, pair_ref, same_at):
    total = got_ref[0].astype(f32)
    for y in range(1, NY):
        total = total + got_ref[y].astype(f32)
    query_ref[...] = rotate(total[:, :HD], tables_ref[0], tables_ref[1]).astype(bf16)
    pair_ref[...] = rotate(total[:, HD:], tables_ref[2], tables_ref[3]).astype(bf16)


def pack_rows_body(spot_ref, own_ref, other_ref, *refs):
    out_ref = refs[-1]
    own = own_ref[...].astype(f32)
    other = other_ref[...].astype(f32)
    at_zero = spot_ref[2] == 0
    wide = jnp.concatenate([jnp.where(at_zero, own, other), jnp.where(at_zero, other, own)], axis=0)
    scale = lax.rsqrt(jnp.mean(wide * wide, axis=-1, keepdims=True) + 1e-05)
    high = scale.astype(bf16).astype(f32)
    lane = lax.broadcasted_iota(jnp.int32, (2 * ROWS, HD), 1)
    tail = jnp.where(lane < HD // 2, high, scale - high).astype(bf16)
    narrow = wide.astype(bf16)
    for place in range(PLANE):
        y = place % NY
        out_ref[place, :, :PART] = narrow[:, y * PART : (y + 1) * PART]
        out_ref[place, :, PART:] = tail


def project_body(spot_ref, x_ref, gain_ref, ring_ref, out_ref, raw_ref, pair_ref):
    raw_ref[...] = x_ref[:, pl.ds(pl.multiple_of(spot_ref[0] * FINE, FINE), FINE)]
    tail = x_ref[:, PART:].astype(f32)
    scale = tail[:, 0:1] + tail[:, HD // 2 : HD // 2 + 1]
    normed = (x_ref[:, :PART].astype(f32) * scale * gain_ref[...].astype(f32)).astype(bf16)
    for y in range(NY):
        for k in range(PART // HD):
            first = PART + k * PIECE
            pair_ref[y * PIECE : (y + 1) * PIECE, k * HD : (k + 1) * HD] = ring_ref[y, first : first + PIECE]
    pair = dot(normed, pair_ref[...], ((1,), (1,))).astype(bf16)
    for y in range(NY):
        out_ref[y, :, :HD] = dot(normed, ring_ref[y, :PART]).astype(bf16)
        out_ref[y, :, HD:] = pair


def rotate(values, cosine, signed_sine):
    lane = lax.broadcasted_iota(jnp.int32, values.shape, 1)
    swapped = jnp.where(lane % 2 == 0, jnp.roll(values, -1, axis=1), jnp.roll(values, 1, axis=1))
    return values * cosine + swapped * signed_sine


def attend_body(spot_ref, query_at, own_at, other_at, across_ref, goal_ref, held_ref, out_ref, held, sems):
    copies = [pltpu.make_async_copy(at, held.at[i], sems.at[i]) for i, at in enumerate((query_at, own_at, other_at))]
    for copy in copies:
        copy.start()
    order = lax.broadcasted_iota(jnp.int32, (TOK, TOK), 0)
    against = lax.broadcasted_iota(jnp.int32, (TOK, TOK), 1)
    across = across_ref[...].astype(f32)
    down = jnp.sum(jnp.where(order == against, across, 0.0), axis=1, keepdims=True)
    allowed = (down == across) & (against <= order)
    for copy in copies:
        copy.wait()
    query = held[0]
    own = held[1].astype(f32)
    other = held[2].astype(f32)
    at_zero = spot_ref[2] == 0
    even = jnp.where(at_zero, own, other)
    odd = jnp.where(at_zero, other, own)
    quarter = lax.broadcasted_iota(jnp.int32, (TOK, HD), 1) // PIECE

    def weave(a, b, c, d):
        return jnp.where(quarter == 0, a, jnp.where(quarter == 1, b, jnp.where(quarter == 2, c, d)))

    def turn(values, by):
        return jnp.roll(values, by * PIECE, axis=1)

    key_block = weave(even, turn(odd, 1), turn(even, 1), turn(odd, 2)).astype(bf16)
    value_block = weave(turn(even, 2), turn(odd, 3), turn(even, 3), odd).astype(bf16)
    scores = dot(query, key_block, ((1,), (1,))) * HD ** (-0.5)
    scores = jnp.where(allowed, scores, masked_score)
    peak = jnp.max(scores, axis=1, keepdims=True)
    powers = jnp.where(allowed, jnp.exp(scores - peak), 0.0)
    prob = (powers / jnp.sum(powers, axis=1, keepdims=True)).astype(bf16)
    mixed = dot(prob, value_block).astype(bf16)
    goal = goal_ref[...].astype(f32)
    for place in range(PLANE):
        start = fine_column(place)
        out_ref[place, :TOK] = mixed
        out_ref[place, TOK:] = fold(goal[:, start : start + FINE]).astype(bf16)


def terms_body(spot_ref, got_ref, w_ref, out_ref, sent_ref, goal_ref):
    goal_ref[...] = jnp.zeros((TOK, FINE), f32)
    total = jnp.zeros((TOK, FINE), f32)
    for place in range(PLANE):
        first = pl.multiple_of(place * 2 * ROWS + spot_ref[2] * ROWS, ROWS)
        goal_ref[pl.ds(first, ROWS), :] = unfold(got_ref[place, TOK:].astype(f32))
    for place in range(0, PLANE, 2):
        pair = (place, place + 1)
        turned = [dot(got_ref[h, :TOK], w_ref[h, :, FINE:]).astype(bf16) for h in pair]
        weights = jnp.concatenate([w_ref[h, :, :FINE] for h in pair], axis=0)
        total = total + dot(jnp.concatenate(turned, axis=1), weights)
    out_ref[...] = total
    sent_ref[...] = (total - goal_ref[...]).astype(bf16)


def grads_body(spot_ref, own_ref, other_ref, x_ref, goal_ref, got_ref, w_ref, out_ref, wide_ref):
    passed = x_ref[...].astype(f32) + (own_ref[...] + other_ref[...].astype(f32))
    wide = passed.astype(bf16).astype(f32)
    wide_ref[...] = wide
    error = (wide - goal_ref[...]).astype(bf16)
    for place in range(0, PLANE, 2):
        pair = (place, place + 1)
        weights = jnp.concatenate([w_ref[h, :, :FINE] for h in pair], axis=0)
        back = dot(error, weights, ((1,), (1,))).astype(bf16)
        for i, h in enumerate(pair):
            part = dot(got_ref[h, :TOK], back[:, i * HD : (i + 1) * HD], ((0,), (0,)))
            out_ref[h, :HD] = part.astype(bf16)
    for place in range(PLANE):
        first = pl.multiple_of(place * 2 * ROWS + spot_ref[2] * ROWS, ROWS)
        out_ref[place, HD:] = fold(wide_ref[pl.ds(first, ROWS), :]).astype(bf16)


def finish_body(got_ref, rows_ref, grad_ref):
    total = got_ref[0, :HD].astype(f32)
    for place in range(1, PLANE):
        total = total + got_ref[place, :HD].astype(f32)
    grad_ref[...] = total
    for place in range(PLANE):
        start = fine_column(place)
        rows_ref[:, start : start + FINE] = unfold(got_ref[place, HD:].astype(f32)).astype(bf16)


def tables(segments, z_at):
    order = jnp.arange(TOK, dtype=jnp.int32)
    same = segments[:, None] == segments[None, :]
    earlier = order[None, :] < order[:, None]
    positions = jnp.sum((same & earlier).astype(jnp.int32), axis=1).astype(f32)
    lane = jnp.arange(HD, dtype=jnp.int32)
    column = lane // PIECE * (NZ * PIECE) + z_at * PIECE + lane % PIECE
    column = jnp.stack([lane, jnp.where(lane < 2 * PIECE, column, 0)])
    turns = jnp.stack([lane >= 0, lane < 2 * PIECE])
    freq = jnp.where(turns, jnp.power(rope_base, -(2.0 * (column // 2).astype(f32)) / HD), 0.0)
    angle = positions[None, :, None] * freq[:, None, :]
    sine = jnp.sin(angle)
    signed = jnp.where(lane[None, None, :] % 2 == 0, -sine, sine)
    both = jnp.stack([jnp.cos(angle), signed], axis=1)
    return both.reshape(4, TOK, HD)


def local(handoff, segment_ids, norm_gain, query_weight, kv_weight, rotation, out_weight, target):
    segments = segment_ids[0]
    w_query = query_weight[0]
    w_pair = kv_weight[0].T
    w_out = out_weight[0]
    goal = target[0]
    x_at, y_at, z_at = lax.axis_index("x"), lax.axis_index("y"), lax.axis_index("z")
    spot = jnp.stack([x_at, y_at, z_at]).astype(jnp.int32)
    gain = lax.dynamic_slice_in_dim(norm_gain, y_at * PART, PART, 1)
    turning = tables(segments, z_at)

    own, other = relay(handoff[0], 0), relay(handoff[0], 1)
    depth = PART + PART * PIECE // HD
    rings = on_core(
        pack_in_body,
        jax.ShapeDtypeStruct((NY, depth, HD), bf16),
        [HELD, HELD],
        0,
        5 * 2**20,
        [pltpu.SemaphoreType.DMA((NY + D // HD,))],
        out_specs=HELD,
        room=60,
    )(w_query, w_pair)
    wo_pack = on_core(
        pack_out_body,
        jax.ShapeDtypeStruct((PLANE, HD, FINE + HD), bf16),
        [HELD, HELD],
        0,
        5 * 2**20,
        [pltpu.SemaphoreType.DMA((2 * PLANE,))],
        out_specs=HELD,
        room=60,
    )(w_out, rotation[0, 0])
    rings = exchange(rings, "y")

    rows = on_core(
        pack_rows_body,
        jax.ShapeDtypeStruct((PLANE, 2 * ROWS, PART + HD), bf16),
        [SMEM, VMEM, VMEM] + [HELD] * 4,
        10**6,
        3 * 2**20,
    )(spot, own, other, rings, turning, wo_pack, gain)
    features = exchange(rows, ("x", "y")).reshape(TOK, PART + HD)

    sent, raw = on_core(
        project_body,
        (jax.ShapeDtypeStruct((NY, TOK, 2 * HD), bf16), jax.ShapeDtypeStruct((TOK, FINE), bf16)),
        [SMEM] + [VMEM] * 3,
        2 * TOK * PART * 5 * HD,
        5 * 2**20,
        [pltpu.VMEM((HD, PART), bf16)],
        out_specs=(VMEM, VMEM),
    )(spot, features, gain, rings)
    got = exchange(sent, "y")

    narrow = jax.ShapeDtypeStruct((TOK, HD), bf16)
    query, pair_own, wo_pack = on_core(
        gather_body,
        (narrow, narrow, jax.ShapeDtypeStruct(wo_pack.shape, bf16)),
        [VMEM, VMEM, HELD],
        10**6,
        2**20,
        out_specs=(VMEM, VMEM, HELD),
        room=60,
        aliases={2: 2},
    )(got, turning, wo_pack)
    pair_other = z_swap(pair_own)
    wo_ring = exchange(wo_pack, ("x", "y"))

    mixed = on_core(
        attend_body,
        jax.ShapeDtypeStruct((PLANE, TOK + ROWS * TILES, HD), bf16),
        [SMEM] + [HELD] * 3 + [VMEM] * 2 + [HELD],
        10**8,
        3 * 2**20,
        [pltpu.VMEM((3, TOK, HD), bf16), pltpu.SemaphoreType.DMA((3,))],
    )(spot, query, pair_own, pair_other, segments[None, :], goal, wo_ring)
    mixed = exchange(mixed, ("x", "y"))

    wide_slice = jax.ShapeDtypeStruct((TOK, FINE), f32)
    terms, terms_sent, goal_slice = on_core(
        terms_body,
        (wide_slice, jax.ShapeDtypeStruct((TOK, FINE), bf16), wide_slice),
        [SMEM, VMEM, VMEM],
        2 * TOK * PLANE * HD * (FINE + HD),
        4 * 2**20,
        out_specs=(VMEM,) * 3,
    )(spot, mixed, wo_ring)
    terms_other = z_swap(terms_sent)

    parts = on_core(
        grads_body,
        jax.ShapeDtypeStruct((PLANE, HD + ROWS * TILES, HD), bf16),
        [SMEM] + [VMEM] * 6,
        2 * TOK * PLANE * HD * (FINE + HD),
        6 * 2**20,
        [pltpu.VMEM((TOK, FINE), f32)],
    )(spot, terms, terms_other, raw, goal_slice, mixed, wo_ring)
    parts = exchange(parts, ("x", "y"))

    out_rows, rot_grad = on_core(
        finish_body,
        (jax.ShapeDtypeStruct((ROWS, D), bf16), jax.ShapeDtypeStruct((HD, HD), f32)),
        [VMEM],
        10**6,
        2**20,
        out_specs=(VMEM, VMEM),
    )(parts)
    return (out_rows[None], rot_grad[None, None])


def solution(mesh):
    devices = mesh.devices
    grid = Mesh(devices.reshape(devices.shape[0], NX, NY, NZ), EVERY)
    head = ("x", "y", "z")
    in_specs = (
        P("phase", head, None),
        P("phase", None),
        P("phase", None),
        P("phase", None, head),
        P("phase", None, head),
        P("phase", head, None, None),
        P("phase", head, None),
        P("phase", head, None),
    )
    out_specs = (P("phase", head, None), P("phase", head, None, None))
    return jax.shard_map(local, mesh=grid, in_specs=in_specs, out_specs=out_specs, check_vma=False)
```

```python
import jax
import jax.numpy as jnp
from jax import lax
from jax.experimental import pallas as pl
from jax.experimental.pallas import tpu as pltpu
from jax.sharding import Mesh, PartitionSpec as P

HD = 128
NX, NY, NZ = 4, 4, 2
PLANE = NX * NY
PIECE = 32
TOK = 256
ROWS = 8
D = 8192
PART = D // NY
FINE = D // PLANE
TILES = FINE // HD
bf16 = jnp.bfloat16
f32 = jnp.float32
rope_base = 500000.0
masked_score = -1e30
EVERY = ("phase", "x", "y", "z")
VMEM = pl.BlockSpec(memory_space=pltpu.VMEM)
SMEM = pl.BlockSpec(memory_space=pltpu.SMEM)
HELD = pl.BlockSpec(memory_space=pl.ANY)


def on_core(body, out_shape, in_specs, flops, moved, scratch=(), out_specs=VMEM, aliases=None):
    return pl.pallas_call(
        body,
        out_shape=out_shape,
        in_specs=in_specs,
        out_specs=out_specs,
        scratch_shapes=list(scratch),
        input_output_aliases=aliases or {},
        compiler_params=pltpu.CompilerParams(vmem_limit_bytes=40 * 2**20),
        cost_estimate=pl.CostEstimate(flops=flops, bytes_accessed=moved, transcendentals=0),
    )


def dot(a, b, dims=((1,), (0,))):
    return lax.dot_general(a, b, (dims, ((), ())), preferred_element_type=f32)


def relay(block, flip):
    phases = lax.axis_size("phase")
    heads = PLANE * NZ
    pairs = [
        (p * heads + h, (p + 1) % phases * heads + (h ^ flip)) for p in range(phases) for h in range(heads)
    ]
    return lax.ppermute(block, EVERY, pairs)


def z_swap(block):
    return lax.ppermute(block, "z", [(0, 1), (1, 0)])


def exchange(blocks, axes):
    return lax.all_to_all(blocks, axes, 0, 0, tiled=True)


def fine_column(place):
    return place % NY * PART + place // NY * FINE


def fold(rows):
    return jnp.concatenate([rows[:, k * HD : (k + 1) * HD] for k in range(TILES)], axis=0)


def unfold(rows):
    return jnp.concatenate([rows[k * ROWS : (k + 1) * ROWS] for k in range(TILES)], axis=1)


def carry_out(copies):
    for copy in copies:
        copy.start()
    for copy in copies:
        copy.wait()


def pack_in_body(wq_at, wkv_at, out_at, sems):
    copies = []
    for y in range(NY):
        start = y * PART
        copies.append((wq_at.at[start : start + PART], out_at.at[y, :PART]))
        for k in range(PART // HD):
            first = PART + k * PIECE
            copies.append((wkv_at.at[:, start + k * HD : start + (k + 1) * HD], out_at.at[y, first : first + PIECE]))
    carry_out([pltpu.make_async_copy(a, b, sems.at[i]) for i, (a, b) in enumerate(copies)])


def pack_out_body(w_at, out_at, sems):
    copies = []
    for place in range(PLANE):
        start = fine_column(place)
        copies.append((w_at.at[:, start : start + FINE], out_at.at[place]))
    carry_out([pltpu.make_async_copy(a, b, sems.at[i]) for i, (a, b) in enumerate(copies)])


def gather_body(got_ref, tables_ref, pack_at, query_ref, pair_ref, same_at):
    total = got_ref[0].astype(f32)
    for y in range(1, NY):
        total = total + got_ref[y].astype(f32)
    query_ref[...] = rotate(total[:, :HD], tables_ref[0], tables_ref[1]).astype(bf16)
    pair_ref[...] = rotate(total[:, HD:], tables_ref[2], tables_ref[3]).astype(bf16)


def pack_rows_body(spot_ref, own_ref, other_ref, *refs):
    out_ref = refs[-1]
    own = own_ref[...].astype(f32)
    other = other_ref[...].astype(f32)
    at_zero = spot_ref[2] == 0
    wide = jnp.concatenate([jnp.where(at_zero, own, other), jnp.where(at_zero, other, own)], axis=0)
    scale = lax.rsqrt(jnp.mean(wide * wide, axis=-1, keepdims=True) + 1e-05)
    high = scale.astype(bf16).astype(f32)
    lane = lax.broadcasted_iota(jnp.int32, (2 * ROWS, HD), 1)
    tail = jnp.where(lane < HD // 2, high, scale - high).astype(bf16)
    narrow = wide.astype(bf16)
    for place in range(PLANE):
        y = place % NY
        out_ref[place, :, :PART] = narrow[:, y * PART : (y + 1) * PART]
        out_ref[place, :, PART:] = tail


def project_body(spot_ref, x_ref, gain_ref, ring_ref, out_ref, raw_ref, pair_ref):
    raw_ref[...] = x_ref[:, pl.ds(pl.multiple_of(spot_ref[0] * FINE, FINE), FINE)]
    tail = x_ref[:, PART:].astype(f32)
    scale = tail[:, 0:1] + tail[:, HD // 2 : HD // 2 + 1]
    normed = (x_ref[:, :PART].astype(f32) * scale * gain_ref[...].astype(f32)).astype(bf16)
    for y in range(NY):
        for k in range(PART // HD):
            first = PART + k * PIECE
            pair_ref[y * PIECE : (y + 1) * PIECE, k * HD : (k + 1) * HD] = ring_ref[y, first : first + PIECE]
    pair = dot(normed, pair_ref[...], ((1,), (1,))).astype(bf16)
    for y in range(NY):
        out_ref[y, :, :HD] = dot(normed, ring_ref[y, :PART]).astype(bf16)
        out_ref[y, :, HD:] = pair


def rotate(values, cosine, signed_sine):
    lane = lax.broadcasted_iota(jnp.int32, values.shape, 1)
    swapped = jnp.where(lane % 2 == 0, jnp.roll(values, -1, axis=1), jnp.roll(values, 1, axis=1))
    return values * cosine + swapped * signed_sine


def attend_body(spot_ref, query_at, own_at, other_at, across_ref, goal_ref, held_ref, out_ref, held, sems):
    copies = [pltpu.make_async_copy(at, held.at[i], sems.at[i]) for i, at in enumerate((query_at, own_at, other_at))]
    for copy in copies:
        copy.start()
    order = lax.broadcasted_iota(jnp.int32, (TOK, TOK), 0)
    against = lax.broadcasted_iota(jnp.int32, (TOK, TOK), 1)
    across = across_ref[...].astype(f32)
    down = jnp.sum(jnp.where(order == against, across, 0.0), axis=1, keepdims=True)
    allowed = (down == across) & (against <= order)
    for copy in copies:
        copy.wait()
    query = held[0]
    own = held[1].astype(f32)
    other = held[2].astype(f32)
    at_zero = spot_ref[2] == 0
    even = jnp.where(at_zero, own, other)
    odd = jnp.where(at_zero, other, own)
    quarter = lax.broadcasted_iota(jnp.int32, (TOK, HD), 1) // PIECE

    def weave(a, b, c, d):
        return jnp.where(quarter == 0, a, jnp.where(quarter == 1, b, jnp.where(quarter == 2, c, d)))

    def turn(values, by):
        return jnp.roll(values, by * PIECE, axis=1)

    key_block = weave(even, turn(odd, 1), turn(even, 1), turn(odd, 2)).astype(bf16)
    value_block = weave(turn(even, 2), turn(odd, 3), turn(even, 3), odd).astype(bf16)
    scores = dot(query, key_block, ((1,), (1,))) * HD ** (-0.5)
    scores = jnp.where(allowed, scores, masked_score)
    peak = jnp.max(scores, axis=1, keepdims=True)
    powers = jnp.where(allowed, jnp.exp(scores - peak), 0.0)
    prob = (powers / jnp.sum(powers, axis=1, keepdims=True)).astype(bf16)
    mixed = dot(prob, value_block).astype(bf16)
    goal = goal_ref[...].astype(f32)
    for place in range(PLANE):
        start = fine_column(place)
        out_ref[place, :TOK] = mixed
        out_ref[place, TOK:] = fold(goal[:, start : start + FINE]).astype(bf16)


def terms_body(spot_ref, got_ref, w_ref, turn_ref, out_ref, sent_ref, goal_ref):
    goal_ref[...] = jnp.zeros((TOK, FINE), f32)
    total = jnp.zeros((TOK, FINE), f32)
    for place in range(PLANE):
        first = pl.multiple_of(place * 2 * ROWS + spot_ref[2] * ROWS, ROWS)
        goal_ref[pl.ds(first, ROWS), :] = unfold(got_ref[place, TOK:].astype(f32))
    for place in range(0, PLANE, 2):
        pair = (place, place + 1)
        turned = [dot(got_ref[h, :TOK], turn_ref[h]).astype(bf16) for h in pair]
        weights = jnp.concatenate([w_ref[h] for h in pair], axis=0)
        total = total + dot(jnp.concatenate(turned, axis=1), weights)
    out_ref[...] = total
    sent_ref[...] = (total - goal_ref[...]).astype(bf16)


def grads_body(spot_ref, own_ref, other_ref, x_ref, goal_ref, got_ref, w_ref, out_ref, wide_ref):
    passed = x_ref[...].astype(f32) + (own_ref[...] + other_ref[...].astype(f32))
    wide = passed.astype(bf16).astype(f32)
    wide_ref[...] = wide
    error = (wide - goal_ref[...]).astype(bf16)
    for place in range(0, PLANE, 2):
        pair = (place, place + 1)
        weights = jnp.concatenate([w_ref[h] for h in pair], axis=0)
        back = dot(error, weights, ((1,), (1,))).astype(bf16)
        for i, h in enumerate(pair):
            part = dot(got_ref[h, :TOK], back[:, i * HD : (i + 1) * HD], ((0,), (0,)))
            out_ref[h, :HD] = part.astype(bf16)
    for place in range(PLANE):
        first = pl.multiple_of(place * 2 * ROWS + spot_ref[2] * ROWS, ROWS)
        out_ref[place, HD:] = fold(wide_ref[pl.ds(first, ROWS), :]).astype(bf16)


def finish_body(got_ref, rows_ref, grad_ref):
    total = got_ref[0, :HD].astype(f32)
    for place in range(1, PLANE):
        total = total + got_ref[place, :HD].astype(f32)
    grad_ref[...] = total
    for place in range(PLANE):
        start = fine_column(place)
        rows_ref[:, start : start + FINE] = unfold(got_ref[place, HD:].astype(f32)).astype(bf16)


def tables(segments, z_at):
    order = jnp.arange(TOK, dtype=jnp.int32)
    same = segments[:, None] == segments[None, :]
    earlier = order[None, :] < order[:, None]
    positions = jnp.sum((same & earlier).astype(jnp.int32), axis=1).astype(f32)
    lane = jnp.arange(HD, dtype=jnp.int32)
    column = lane // PIECE * (NZ * PIECE) + z_at * PIECE + lane % PIECE
    column = jnp.stack([lane, jnp.where(lane < 2 * PIECE, column, 0)])
    turns = jnp.stack([lane >= 0, lane < 2 * PIECE])
    freq = jnp.where(turns, jnp.power(rope_base, -(2.0 * (column // 2).astype(f32)) / HD), 0.0)
    angle = positions[None, :, None] * freq[:, None, :]
    sine = jnp.sin(angle)
    signed = jnp.where(lane[None, None, :] % 2 == 0, -sine, sine)
    both = jnp.stack([jnp.cos(angle), signed], axis=1)
    return both.reshape(4, TOK, HD)


def local(handoff, segment_ids, norm_gain, query_weight, kv_weight, rotation, out_weight, target):
    segments = segment_ids[0]
    w_query = query_weight[0]
    w_pair = kv_weight[0].T
    w_out = out_weight[0]
    goal = target[0]
    x_at, y_at, z_at = lax.axis_index("x"), lax.axis_index("y"), lax.axis_index("z")
    spot = jnp.stack([x_at, y_at, z_at]).astype(jnp.int32)
    gain = lax.dynamic_slice_in_dim(norm_gain, y_at * PART, PART, 1)
    turning = tables(segments, z_at)

    own, other = relay(handoff[0], 0), relay(handoff[0], 1)
    depth = PART + PART * PIECE // HD
    rings = on_core(
        pack_in_body,
        jax.ShapeDtypeStruct((NY, depth, HD), bf16),
        [HELD, HELD],
        0,
        5 * 2**20,
        [pltpu.SemaphoreType.DMA((NY + D // HD,))],
        out_specs=HELD,
    )(w_query, w_pair)
    wo_pack = on_core(
        pack_out_body,
        jax.ShapeDtypeStruct((PLANE, HD, FINE), bf16),
        [HELD],
        0,
        4 * 2**20,
        [pltpu.SemaphoreType.DMA((PLANE,))],
        out_specs=HELD,
    )(w_out)
    turns = lax.all_gather(rotation[0, 0], ("x", "y"))
    rings = exchange(rings, "y")

    rows = on_core(
        pack_rows_body,
        jax.ShapeDtypeStruct((PLANE, 2 * ROWS, PART + HD), bf16),
        [SMEM, VMEM, VMEM] + [HELD] * 4,
        10**6,
        3 * 2**20,
    )(spot, own, other, rings, turning, wo_pack, gain)
    features = exchange(rows, ("x", "y")).reshape(TOK, PART + HD)

    sent, raw = on_core(
        project_body,
        (jax.ShapeDtypeStruct((NY, TOK, 2 * HD), bf16), jax.ShapeDtypeStruct((TOK, FINE), bf16)),
        [SMEM] + [VMEM] * 3,
        2 * TOK * PART * 5 * HD,
        5 * 2**20,
        [pltpu.VMEM((HD, PART), bf16)],
        out_specs=(VMEM, VMEM),
    )(spot, features, gain, rings)
    got = exchange(sent, "y")

    narrow = jax.ShapeDtypeStruct((TOK, HD), bf16)
    query, pair_own, wo_pack = on_core(
        gather_body,
        (narrow, narrow, jax.ShapeDtypeStruct(wo_pack.shape, bf16)),
        [VMEM, VMEM, HELD],
        10**6,
        2**20,
        out_specs=(VMEM, VMEM, HELD),
        aliases={2: 2},
    )(got, turning, wo_pack)
    pair_other = z_swap(pair_own)
    wo_ring = exchange(wo_pack, ("x", "y"))

    mixed = on_core(
        attend_body,
        jax.ShapeDtypeStruct((PLANE, TOK + ROWS * TILES, HD), bf16),
        [SMEM] + [HELD] * 3 + [VMEM] * 2 + [HELD],
        10**8,
        3 * 2**20,
        [pltpu.VMEM((3, TOK, HD), bf16), pltpu.SemaphoreType.DMA((3,))],
    )(spot, query, pair_own, pair_other, segments[None, :], goal, wo_ring)
    mixed = exchange(mixed, ("x", "y"))

    wide_slice = jax.ShapeDtypeStruct((TOK, FINE), f32)
    terms, terms_sent, goal_slice = on_core(
        terms_body,
        (wide_slice, jax.ShapeDtypeStruct((TOK, FINE), bf16), wide_slice),
        [SMEM, VMEM, VMEM, VMEM],
        2 * TOK * PLANE * HD * (FINE + HD),
        4 * 2**20,
        out_specs=(VMEM,) * 3,
    )(spot, mixed, wo_ring, turns)
    terms_other = z_swap(terms_sent)

    parts = on_core(
        grads_body,
        jax.ShapeDtypeStruct((PLANE, HD + ROWS * TILES, HD), bf16),
        [SMEM] + [VMEM] * 6,
        2 * TOK * PLANE * HD * (FINE + HD),
        6 * 2**20,
        [pltpu.VMEM((TOK, FINE), f32)],
    )(spot, terms, terms_other, raw, goal_slice, mixed, wo_ring)
    parts = exchange(parts, ("x", "y"))

    out_rows, rot_grad = on_core(
        finish_body,
        (jax.ShapeDtypeStruct((ROWS, D), bf16), jax.ShapeDtypeStruct((HD, HD), f32)),
        [VMEM],
        10**6,
        2**20,
        out_specs=(VMEM, VMEM),
    )(parts)
    return (out_rows[None], rot_grad[None, None])


def solution(mesh):
    devices = mesh.devices
    grid = Mesh(devices.reshape(devices.shape[0], NX, NY, NZ), EVERY)
    head = ("x", "y", "z")
    in_specs = (
        P("phase", head, None),
        P("phase", None),
        P("phase", None),
        P("phase", None, head),
        P("phase", None, head),
        P("phase", head, None, None),
        P("phase", head, None),
        P("phase", head, None),
    )
    out_specs = (P("phase", head, None), P("phase", head, None, None))
    return jax.shard_map(local, mesh=grid, in_specs=in_specs, out_specs=out_specs, check_vma=False)
```

```python
import jax
import jax.numpy as jnp
from jax import lax
from jax.experimental import pallas as pl
from jax.experimental.pallas import tpu as pltpu
from jax.sharding import Mesh, PartitionSpec as P

HD = 128
NX, NY, NZ = 4, 4, 2
PLANE = NX * NY
PIECE = 32
TOK = 256
ROWS = 8
D = 8192
PART = D // NY
FINE = D // PLANE
TILES = FINE // HD
bf16 = jnp.bfloat16
f32 = jnp.float32
rope_base = 500000.0
masked_score = -1e30
EVERY = ("phase", "x", "y", "z")
VMEM = pl.BlockSpec(memory_space=pltpu.VMEM)
SMEM = pl.BlockSpec(memory_space=pltpu.SMEM)
HELD = pl.BlockSpec(memory_space=pl.ANY)


def on_core(body, out_shape, in_specs, flops, moved, scratch=(), out_specs=VMEM, aliases=None):
    return pl.pallas_call(
        body,
        out_shape=out_shape,
        in_specs=in_specs,
        out_specs=out_specs,
        scratch_shapes=list(scratch),
        input_output_aliases=aliases or {},
        compiler_params=pltpu.CompilerParams(vmem_limit_bytes=40 * 2**20),
        cost_estimate=pl.CostEstimate(flops=flops, bytes_accessed=moved, transcendentals=0),
    )


def dot(a, b, dims=((1,), (0,))):
    return lax.dot_general(a, b, (dims, ((), ())), preferred_element_type=f32)


def relay(block, flip):
    phases = lax.axis_size("phase")
    heads = PLANE * NZ
    pairs = [
        (p * heads + h, (p + 1) % phases * heads + (h ^ flip)) for p in range(phases) for h in range(heads)
    ]
    return lax.ppermute(block, EVERY, pairs)


def z_swap(block):
    return lax.ppermute(block, "z", [(0, 1), (1, 0)])


def exchange(blocks, axes):
    return lax.all_to_all(blocks, axes, 0, 0, tiled=True)


def fine_column(place):
    return place % NY * PART + place // NY * FINE


def fold(rows):
    return jnp.concatenate([rows[:, k * HD : (k + 1) * HD] for k in range(TILES)], axis=0)


def unfold(rows):
    return jnp.concatenate([rows[k * ROWS : (k + 1) * ROWS] for k in range(TILES)], axis=1)


def carry_out(copies):
    for copy in copies:
        copy.start()
    for copy in copies:
        copy.wait()


def pack_in_body(wq_ref, wkv_ref, out_ref):
    for y in range(NY):
        start = y * PART
        out_ref[y, :PART] = wq_ref[start : start + PART]
        for k in range(PART // HD):
            first = PART + k * PIECE
            out_ref[y, first : first + PIECE] = wkv_ref[:, start + k * HD : start + (k + 1) * HD]


def pack_out_body(w_at, turn_at, out_at, sems):
    copies = []
    for place in range(PLANE):
        start = fine_column(place)
        copies.append((w_at.at[:, start : start + FINE], out_at.at[place, :, :FINE]))
        copies.append((turn_at, out_at.at[place, :, FINE:]))
    carry_out([pltpu.make_async_copy(a, b, sems.at[i]) for i, (a, b) in enumerate(copies)])


def gather_body(got_ref, tables_ref, pack_at, query_ref, pair_ref, same_at):
    total = got_ref[0].astype(f32)
    for y in range(1, NY):
        total = total + got_ref[y].astype(f32)
    query_ref[...] = rotate(total[:, :HD], tables_ref[0], tables_ref[1]).astype(bf16)
    pair_ref[...] = rotate(total[:, HD:], tables_ref[2], tables_ref[3]).astype(bf16)


def pack_rows_body(spot_ref, own_ref, other_ref, *refs):
    out_ref = refs[-1]
    own = own_ref[...].astype(f32)
    other = other_ref[...].astype(f32)
    at_zero = spot_ref[2] == 0
    wide = jnp.concatenate([jnp.where(at_zero, own, other), jnp.where(at_zero, other, own)], axis=0)
    scale = lax.rsqrt(jnp.mean(wide * wide, axis=-1, keepdims=True) + 1e-05)
    high = scale.astype(bf16).astype(f32)
    lane = lax.broadcasted_iota(jnp.int32, (2 * ROWS, HD), 1)
    tail = jnp.where(lane < HD // 2, high, scale - high).astype(bf16)
    narrow = wide.astype(bf16)
    for place in range(PLANE):
        y = place % NY
        out_ref[place, :, :PART] = narrow[:, y * PART : (y + 1) * PART]
        out_ref[place, :, PART:] = tail


def project_body(spot_ref, x_ref, gain_ref, ring_ref, out_ref, raw_ref, pair_ref):
    raw_ref[...] = x_ref[:, pl.ds(pl.multiple_of(spot_ref[0] * FINE, FINE), FINE)]
    tail = x_ref[:, PART:].astype(f32)
    scale = tail[:, 0:1] + tail[:, HD // 2 : HD // 2 + 1]
    normed = (x_ref[:, :PART].astype(f32) * scale * gain_ref[...].astype(f32)).astype(bf16)
    for y in range(NY):
        for k in range(PART // HD):
            first = PART + k * PIECE
            pair_ref[y * PIECE : (y + 1) * PIECE, k * HD : (k + 1) * HD] = ring_ref[y, first : first + PIECE]
    pair = dot(normed, pair_ref[...], ((1,), (1,))).astype(bf16)
    for y in range(0, NY, 2):
        weights = jnp.concatenate([ring_ref[y, :PART], ring_ref[y + 1, :PART]], axis=1)
        queries = dot(normed, weights).astype(bf16)
        for i in range(2):
            out_ref[y + i, :, :HD] = queries[:, i * HD : (i + 1) * HD]
            out_ref[y + i, :, HD:] = pair


def rotate(values, cosine, signed_sine):
    lane = lax.broadcasted_iota(jnp.int32, values.shape, 1)
    swapped = jnp.where(lane % 2 == 0, jnp.roll(values, -1, axis=1), jnp.roll(values, 1, axis=1))
    return values * cosine + swapped * signed_sine


def attend_body(spot_ref, query_at, own_at, other_at, across_ref, goal_ref, held_ref, out_ref, held, sems):
    copies = [pltpu.make_async_copy(at, held.at[i], sems.at[i]) for i, at in enumerate((query_at, own_at, other_at))]
    for copy in copies:
        copy.start()
    order = lax.broadcasted_iota(jnp.int32, (TOK, TOK), 0)
    against = lax.broadcasted_iota(jnp.int32, (TOK, TOK), 1)
    across = across_ref[...].astype(f32)
    down = jnp.sum(jnp.where(order == against, across, 0.0), axis=1, keepdims=True)
    allowed = (down == across) & (against <= order)
    for copy in copies:
        copy.wait()
    query = held[0]
    own = held[1].astype(f32)
    other = held[2].astype(f32)
    at_zero = spot_ref[2] == 0
    even = jnp.where(at_zero, own, other)
    odd = jnp.where(at_zero, other, own)
    quarter = lax.broadcasted_iota(jnp.int32, (TOK, HD), 1) // PIECE

    def weave(a, b, c, d):
        return jnp.where(quarter == 0, a, jnp.where(quarter == 1, b, jnp.where(quarter == 2, c, d)))

    def turn(values, by):
        return jnp.roll(values, by * PIECE, axis=1)

    key_block = weave(even, turn(odd, 1), turn(even, 1), turn(odd, 2)).astype(bf16)
    value_block = weave(turn(even, 2), turn(odd, 3), turn(even, 3), odd).astype(bf16)
    scores = dot(query, key_block, ((1,), (1,))) * HD ** (-0.5)
    scores = jnp.where(allowed, scores, masked_score)
    peak = jnp.max(scores, axis=1, keepdims=True)
    powers = jnp.where(allowed, jnp.exp(scores - peak), 0.0)
    prob = (powers / jnp.sum(powers, axis=1, keepdims=True)).astype(bf16)
    mixed = dot(prob, value_block).astype(bf16)
    goal = goal_ref[...].astype(f32)
    for place in range(PLANE):
        start = fine_column(place)
        out_ref[place, :TOK] = mixed
        out_ref[place, TOK:] = fold(goal[:, start : start + FINE]).astype(bf16)


def terms_body(spot_ref, got_ref, w_ref, out_ref, sent_ref, goal_ref):
    goal_ref[...] = jnp.zeros((TOK, FINE), f32)
    total = jnp.zeros((TOK, FINE), f32)
    for place in range(PLANE):
        first = pl.multiple_of(place * 2 * ROWS + spot_ref[2] * ROWS, ROWS)
        goal_ref[pl.ds(first, ROWS), :] = unfold(got_ref[place, TOK:].astype(f32))
    for place in range(0, PLANE, 2):
        pair = (place, place + 1)
        turned = [dot(got_ref[h, :TOK], w_ref[h, :, FINE:]).astype(bf16) for h in pair]
        weights = jnp.concatenate([w_ref[h, :, :FINE] for h in pair], axis=0)
        total = total + dot(jnp.concatenate(turned, axis=1), weights)
    out_ref[...] = total
    sent_ref[...] = (total - goal_ref[...]).astype(bf16)


def grads_body(spot_ref, own_ref, other_ref, x_ref, goal_ref, got_ref, w_ref, out_ref, wide_ref):
    passed = x_ref[...].astype(f32) + (own_ref[...] + other_ref[...].astype(f32))
    wide = passed.astype(bf16).astype(f32)
    wide_ref[...] = wide
    error = (wide - goal_ref[...]).astype(bf16)
    for place in range(0, PLANE, 2):
        pair = (place, place + 1)
        weights = jnp.concatenate([w_ref[h, :, :FINE] for h in pair], axis=0)
        back = dot(error, weights, ((1,), (1,))).astype(bf16)
        for i, h in enumerate(pair):
            part = dot(got_ref[h, :TOK], back[:, i * HD : (i + 1) * HD], ((0,), (0,)))
            out_ref[h, :HD] = part.astype(bf16)
    for place in range(PLANE):
        first = pl.multiple_of(place * 2 * ROWS + spot_ref[2] * ROWS, ROWS)
        out_ref[place, HD:] = fold(wide_ref[pl.ds(first, ROWS), :]).astype(bf16)


def finish_body(got_ref, rows_ref, grad_ref):
    total = got_ref[0, :HD].astype(f32)
    for place in range(1, PLANE):
        total = total + got_ref[place, :HD].astype(f32)
    grad_ref[...] = total
    for place in range(PLANE):
        start = fine_column(place)
        rows_ref[:, start : start + FINE] = unfold(got_ref[place, HD:].astype(f32)).astype(bf16)


def tables(segments, z_at):
    order = jnp.arange(TOK, dtype=jnp.int32)
    same = segments[:, None] == segments[None, :]
    earlier = order[None, :] < order[:, None]
    positions = jnp.sum((same & earlier).astype(jnp.int32), axis=1).astype(f32)
    lane = jnp.arange(HD, dtype=jnp.int32)
    column = lane // PIECE * (NZ * PIECE) + z_at * PIECE + lane % PIECE
    column = jnp.stack([lane, jnp.where(lane < 2 * PIECE, column, 0)])
    turns = jnp.stack([lane >= 0, lane < 2 * PIECE])
    freq = jnp.where(turns, jnp.power(rope_base, -(2.0 * (column // 2).astype(f32)) / HD), 0.0)
    angle = positions[None, :, None] * freq[:, None, :]
    sine = jnp.sin(angle)
    signed = jnp.where(lane[None, None, :] % 2 == 0, -sine, sine)
    both = jnp.stack([jnp.cos(angle), signed], axis=1)
    return both.reshape(4, TOK, HD)


def local(handoff, segment_ids, norm_gain, query_weight, kv_weight, rotation, out_weight, target):
    segments = segment_ids[0]
    w_query = query_weight[0]
    w_pair = kv_weight[0].T
    w_out = out_weight[0]
    goal = target[0]
    x_at, y_at, z_at = lax.axis_index("x"), lax.axis_index("y"), lax.axis_index("z")
    spot = jnp.stack([x_at, y_at, z_at]).astype(jnp.int32)
    gain = lax.dynamic_slice_in_dim(norm_gain, y_at * PART, PART, 1)
    turning = tables(segments, z_at)

    own, other = relay(handoff[0], 0), relay(handoff[0], 1)
    depth = PART + PART * PIECE // HD
    rings = on_core(
        pack_in_body,
        jax.ShapeDtypeStruct((NY, depth, HD), bf16),
        [VMEM, VMEM],
        0,
        5 * 2**20,
    )(w_query, w_pair)
    wo_pack = on_core(
        pack_out_body,
        jax.ShapeDtypeStruct((PLANE, HD, FINE + HD), bf16),
        [HELD, HELD],
        0,
        5 * 2**20,
        [pltpu.SemaphoreType.DMA((2 * PLANE,))],
        out_specs=HELD,
    )(w_out, rotation[0, 0])
    rings = exchange(rings, "y")

    rows = on_core(
        pack_rows_body,
        jax.ShapeDtypeStruct((PLANE, 2 * ROWS, PART + HD), bf16),
        [SMEM, VMEM, VMEM] + [HELD] * 4,
        10**6,
        3 * 2**20,
    )(spot, own, other, rings, turning, wo_pack, gain)
    features = exchange(rows, ("x", "y")).reshape(TOK, PART + HD)

    sent, raw = on_core(
        project_body,
        (jax.ShapeDtypeStruct((NY, TOK, 2 * HD), bf16), jax.ShapeDtypeStruct((TOK, FINE), bf16)),
        [SMEM] + [VMEM] * 3,
        2 * TOK * PART * 5 * HD,
        5 * 2**20,
        [pltpu.VMEM((HD, PART), bf16)],
        out_specs=(VMEM, VMEM),
    )(spot, features, gain, rings)
    got = exchange(sent, "y")

    narrow = jax.ShapeDtypeStruct((TOK, HD), bf16)
    query, pair_own, wo_pack = on_core(
        gather_body,
        (narrow, narrow, jax.ShapeDtypeStruct(wo_pack.shape, bf16)),
        [VMEM, VMEM, HELD],
        10**6,
        2**20,
        out_specs=(VMEM, VMEM, HELD),
        aliases={2: 2},
    )(got, turning, wo_pack)
    pair_other = z_swap(pair_own)
    wo_ring = exchange(wo_pack, ("x", "y"))

    mixed = on_core(
        attend_body,
        jax.ShapeDtypeStruct((PLANE, TOK + ROWS * TILES, HD), bf16),
        [SMEM] + [HELD] * 3 + [VMEM] * 2 + [HELD],
        10**8,
        3 * 2**20,
        [pltpu.VMEM((3, TOK, HD), bf16), pltpu.SemaphoreType.DMA((3,))],
    )(spot, query, pair_own, pair_other, segments[None, :], goal, wo_ring)
    mixed = exchange(mixed, ("x", "y"))

    wide_slice = jax.ShapeDtypeStruct((TOK, FINE), f32)
    terms, terms_sent, goal_slice = on_core(
        terms_body,
        (wide_slice, jax.ShapeDtypeStruct((TOK, FINE), bf16), wide_slice),
        [SMEM, VMEM, VMEM],
        2 * TOK * PLANE * HD * (FINE + HD),
        4 * 2**20,
        out_specs=(VMEM,) * 3,
    )(spot, mixed, wo_ring)
    terms_other = z_swap(terms_sent)

    parts = on_core(
        grads_body,
        jax.ShapeDtypeStruct((PLANE, HD + ROWS * TILES, HD), bf16),
        [SMEM] + [VMEM] * 6,
        2 * TOK * PLANE * HD * (FINE + HD),
        6 * 2**20,
        [pltpu.VMEM((TOK, FINE), f32)],
    )(spot, terms, terms_other, raw, goal_slice, mixed, wo_ring)
    parts = exchange(parts, ("x", "y"))

    out_rows, rot_grad = on_core(
        finish_body,
        (jax.ShapeDtypeStruct((ROWS, D), bf16), jax.ShapeDtypeStruct((HD, HD), f32)),
        [VMEM],
        10**6,
        2**20,
        out_specs=(VMEM, VMEM),
    )(parts)
    return (out_rows[None], rot_grad[None, None])


def solution(mesh):
    devices = mesh.devices
    grid = Mesh(devices.reshape(devices.shape[0], NX, NY, NZ), EVERY)
    head = ("x", "y", "z")
    in_specs = (
        P("phase", head, None),
        P("phase", None),
        P("phase", None),
        P("phase", None, head),
        P("phase", None, head),
        P("phase", head, None, None),
        P("phase", head, None),
        P("phase", head, None),
    )
    out_specs = (P("phase", head, None), P("phase", head, None, None))
    return jax.shard_map(local, mesh=grid, in_specs=in_specs, out_specs=out_specs, check_vma=False)
```
